32 devices in a mesh: ctx: 8 (over z, x), head: 4 (over y, core).
Axes of the slice: x: 2, y: 2, z: 4, core: 2. Of those that a mesh axis runs over, the one named last changes fastest.
Arguments:
- queries: bfloat16 [2048, 2560], P('ctx', 'head'), may hold values from -130 to 130
- keys: bfloat16 [2048, 2560], P('ctx', 'head'), may hold values from -7 to 7
- values: bfloat16 [2048, 2560], P('ctx', 'head'), may hold values from -6 to 6
- out_weight: bfloat16 [2560, 5120], P('head'), may hold values from -0.125 to 0.125
- reward_grad: bfloat16 [2048, 5120], P('ctx', 'head'), may hold values from -6 to 6
- tile_mask: int32 [16, 10], replicated, may hold values from 0 to 1, as said below
Outputs:
- grad_queries: bfloat16 [2048, 2560], P('ctx', 'head')
- grad_keys: bfloat16 [2048, 2560], P('ctx', 'head')
- grad_values: bfloat16 [2048, 2560], P('ctx', 'head')
The draws below stay inside these ranges and needn't reach their ends.
Inputs may be any that keep to these rules, and one draw needn't show every extreme that they name: `tile_mask`: entries are 0 or 1. The column 4 + (row % 2), a query tile's own tile, is always 1; columns that name a tile outside the sequence are 0.
All inputs are finite; a program needn't handle non-finite values.
Results may differ from the reference program's by a relative error of at most 0.033.
Values may be sent and summed in bfloat16 or wider, within the bound.
No kernel may reach another device: no remote copies, remote signals or barrier semaphores. Data moves between devices by JAX's collectives and lax.ppermute only.
A program may use at most 128 MiB of HBM per device.

```python
import math
import jax
import jax.numpy as jnp
from jax import lax

D = 5120
HEAD_DIM = 128
HEADS = 20
TILE = 128
SPAN = 2
TOK_DEV = 256
TOKENS = 2048
TILES_DEV = 2
TILES = 16
WIN_TILES = 10


def shared_query_key(key):
    base = jax.random.fold_in(key, 11)
    key_q, key_k = jax.random.split(base, 2)
    feat_width = HEADS * HEAD_DIM
    full_shape = (TOKENS, feat_width)
    query_draw = jnp.clip(jax.random.normal(key_q, full_shape, jnp.float32), -6.0, 6.0)
    key_draw = jnp.clip(jax.random.normal(key_k, full_shape, jnp.float32), -6.0, 6.0)
    return (query_draw, key_draw)


def draw_queries(key, part):
    return shared_query_key(key)[0].astype(jnp.bfloat16)


def draw_keys(key, part):
    return shared_query_key(key)[1].astype(jnp.bfloat16)


def draw_tile_mask(key, part):
    base = jax.random.fold_in(key, 23)
    key_level, key_tiles = jax.random.split(base, 2)
    block_count = TOKENS // TOK_DEV
    level = jax.random.randint(key_level, (block_count,), 1, 9)
    draws = jax.random.randint(key_tiles, (TILES, WIN_TILES), 0, 8)
    tile_idx = jnp.arange(TILES, dtype=jnp.int32)
    block_of = tile_idx // TILES_DEV
    local_tile = tile_idx % TILES_DEV
    column_idx = jnp.arange(WIN_TILES, dtype=jnp.int32)
    target = (block_of[:, None] - SPAN) * TILES_DEV + column_idx[None, :]
    in_range = (target >= 0) & (target < TILES)
    chosen = draws < level[block_of][:, None]
    diagonal = column_idx[None, :] == SPAN * TILES_DEV + local_tile[:, None]
    return jnp.where(diagonal, 1, jnp.where(chosen & in_range, 1, 0)).astype(jnp.int32)


def shard_levels(stream_key, dims, shards, smallest, high):
    level, own = 1.0, jax.random.fold_in(stream_key, 6)
    for axis_at, shards_of in shards:
        steps = jnp.exp(jax.random.uniform(jax.random.fold_in(own, axis_at), (shards_of,), jnp.float32, smallest / len(shards), high / len(shards)))
        level = level * jnp.repeat(steps, dims[axis_at] // shards_of).reshape([-1 if axis == axis_at else 1 for axis in range(len(dims))])
    return level


def normal_values(rng, shape, deviation, reach, cuts=(), held_as=jnp.bfloat16):
    entries = jax.random.normal(rng, shape, jnp.float32) * deviation
    if len(cuts) > 0:
        entries = shard_levels(rng, shape, cuts, -0.22, 0.18) * entries
    return jnp.clip(entries, min=-reach, max=reach).astype(held_as)


def setup_inputs(seed: int = 0) -> dict:
    splits = jax.random.split(jax.random.key(seed), 7)
    return {
        "queries": draw_queries(jax.random.fold_in(splits[6], 71), 0),
        "keys": draw_keys(jax.random.fold_in(splits[6], 71), 0),
        "values": normal_values(splits[2], (TOKENS, HEADS * HEAD_DIM), 1.0, 6.0, ((0, 8), (1, 4))),
        "out_weight": normal_values(splits[3], (HEADS * HEAD_DIM, D), (HEADS * HEAD_DIM) ** -0.5, 0.125, ((0, 4),)),
        "reward_grad": normal_values(splits[4], (TOKENS, D), 1.0, 6.0, ((0, 8), (1, 4))),
        "tile_mask": draw_tile_mask(jax.random.fold_in(splits[6], 71), 0),
    }


def rounded(array_in):
    return lax.optimization_barrier(array_in.astype(jnp.bfloat16)).astype(jnp.float32)

def attend_block(query_blk, key_win, value_win, grad_blk, live_pairs, score_scale):
    scores = jnp.einsum('qhd,khd->hqk', query_blk, key_win) * score_scale
    live_three = live_pairs[None, :, :]
    row_max = lax.optimization_barrier(jnp.max(jnp.where(live_three, scores, -jnp.inf), axis=-1, keepdims=True))
    weights = jnp.where(live_three, jnp.exp(scores - row_max), 0.0)
    totals = lax.optimization_barrier(jnp.sum(weights, axis=-1, keepdims=True))
    attn_out = rounded(jnp.einsum('hqk,khd->hqd', rounded(weights), value_win) / totals)
    grad_heads = jnp.transpose(grad_blk, (1, 0, 2))
    delta = lax.optimization_barrier(jnp.sum(grad_heads * attn_out, axis=-1, keepdims=True))
    probs = weights / totals
    grad_value_win = jnp.einsum('hqk,hqd->khd', rounded(probs), grad_heads)
    dprobs = jnp.einsum('hqd,khd->hqk', grad_heads, value_win)
    dscores = rounded(probs * (dprobs - delta))
    grad_query_blk = (jnp.einsum('hqk,khd->qhd', dscores, key_win) * score_scale).astype(jnp.bfloat16)
    grad_key_win = jnp.einsum('hqk,qhd->khd', dscores, query_blk) * score_scale
    return (grad_query_blk, grad_key_win, grad_value_win)

def reference(queries, keys, values, out_weight, reward_grad, tile_mask):
    feat_width = HEADS * HEAD_DIM
    score_scale = 1.0 / math.sqrt(HEAD_DIM)
    block_count = TOKENS // TOK_DEV
    window_len = (2 * SPAN + 1) * TOK_DEV
    margin = SPAN * TOK_DEV
    d_out = jnp.dot(reward_grad, out_weight.T, preferred_element_type=jnp.float32).astype(jnp.bfloat16)
    key_padded = jnp.pad(keys, ((margin, margin), (0, 0)))
    value_padded = jnp.pad(values, ((margin, margin), (0, 0)))
    columns = jnp.arange(WIN_TILES, dtype=jnp.int32)

    def one_block(carry, block_idx):
        grad_key_all, grad_value_all = carry
        first = (block_idx * TOK_DEV).astype(jnp.int32)
        query_blk = lax.dynamic_slice_in_dim(queries, first, TOK_DEV, 0).astype(jnp.float32).reshape(TOK_DEV, HEADS, HEAD_DIM)
        key_win = lax.dynamic_slice_in_dim(key_padded, first, window_len, 0).astype(jnp.float32).reshape(window_len, HEADS, HEAD_DIM)
        value_win = lax.dynamic_slice_in_dim(value_padded, first, window_len, 0).astype(jnp.float32).reshape(window_len, HEADS, HEAD_DIM)
        grad_blk = lax.dynamic_slice_in_dim(d_out, first, TOK_DEV, 0).astype(jnp.float32).reshape(TOK_DEV, HEADS, HEAD_DIM)
        mask_rows = lax.dynamic_slice_in_dim(tile_mask, (block_idx * TILES_DEV).astype(jnp.int32), TILES_DEV, 0)
        target = (block_idx - SPAN).astype(jnp.int32) * TILES_DEV + columns
        tile_live = (mask_rows > 0) & ((target >= 0) & (target < TILES))[None, :]
        live_pairs = jnp.broadcast_to(tile_live[:, None, :, None], (TILES_DEV, TILE, WIN_TILES, TILE)).reshape(TOK_DEV, window_len)
        grad_query_blk, grad_key_win, grad_value_win = attend_block(query_blk, key_win, value_win, grad_blk, live_pairs, score_scale)
        grad_key_all = lax.dynamic_update_slice_in_dim(grad_key_all, lax.dynamic_slice_in_dim(grad_key_all, first, window_len, 0) + grad_key_win.reshape(window_len, feat_width), first, 0)
        grad_value_all = lax.dynamic_update_slice_in_dim(grad_value_all, lax.dynamic_slice_in_dim(grad_value_all, first, window_len, 0) + grad_value_win.reshape(window_len, feat_width), first, 0)
        return ((grad_key_all, grad_value_all), grad_query_blk.reshape(TOK_DEV, feat_width))
    start_zero = jnp.zeros((TOKENS + 2 * margin, feat_width), jnp.float32)
    (grad_key_all, grad_value_all), grad_query_parts = lax.scan(one_block, (start_zero, start_zero), jnp.arange(block_count, dtype=jnp.int32))
    grad_queries = grad_query_parts.reshape(TOKENS, feat_width)
    grad_keys = grad_key_all[margin:margin + TOKENS].astype(jnp.bfloat16)
    grad_values = grad_value_all[margin:margin + TOKENS].astype(jnp.bfloat16)
    return (grad_queries, grad_keys, grad_values)
```

```python
import functools
import math

import jax
import jax.numpy as jnp
from jax import lax
from jax.experimental import pallas as pl
from jax.experimental.pallas import tpu as pltpu
from jax.sharding import PartitionSpec as P

HEAD_DIM = 128
TILE = 128
SPAN = 2
STAT_ROWS = 16
SCALE = 1.0 / math.sqrt(HEAD_DIM)
SCALE_LOG2 = SCALE * math.log2(math.e)
BOTH = ("ctx", "head")
NT = (((1,), (1,)), ((), ()))
TN = (((0,), (0,)), ((), ()))
NN = (((1,), (0,)), ((), ()))
VMEM_LIMIT = 48 * 1024 * 1024


def dot(a, b, dims):
    return lax.dot_general(a, b, dims, preferred_element_type=jnp.float32)


def send(array, rule):
    n_ctx, n_head = lax.axis_size("ctx"), lax.axis_size("head")
    pairs = []
    for c in range(n_ctx):
        for h in range(n_head):
            to = rule(c, h)
            if to is not None and 0 <= to[0] < n_ctx:
                pairs.append((c * n_head + h, to[0] * n_head + to[1]))
    return lax.ppermute(array, BOTH, pairs)


def pair_up(c, h):
    return (c ^ 1, h)


def upward(c, h):
    return (c + 2, h)


def downward(c, h):
    return (c - 2, h)


def across(c, h):
    return (c + 1, h) if c & 1 else (c - 1, h)


def forward(c, h):
    if h & 1:
        return (c ^ 1, h)
    return (c - 2, h) if c & 1 else (c + 2, h)


def after(value, *others):
    return lax.optimization_barrier((value,) + others)[0]


def matmul_kernel(first, last, order_ref, w_a, w_b, g_a, g_b, *rest):
    if first:
        out_ref, acc_ref = rest
    else:
        begin_ref, out_ref, acc_ref = rest
    step = pl.program_id(0)
    part = dot(w_a[...], g_a[...], NT) + dot(w_b[...], g_b[...], NT)

    @pl.when(step == 0)
    def _():
        acc_ref[...] = part if first else part + begin_ref[...]

    @pl.when(step > 0)
    def _():
        acc_ref[...] += part

    @pl.when(step == pl.num_programs(0) - 1)
    def _():
        out_ref[...] = acc_ref[...].astype(out_ref.dtype)


def partial_out(order, out_weight, g_a, g_b, begin, dtype):
    feat, width = out_weight.shape
    rows, cols = g_a.shape
    steps = 5
    block = cols // steps
    first = begin is None
    in_specs = [
        pl.BlockSpec((feat, block), lambda s, o: (0, o[0] * steps + s)),
        pl.BlockSpec((feat, block), lambda s, o: (0, o[1] * steps + s)),
        pl.BlockSpec((rows, block), lambda s, o: (0, s)),
        pl.BlockSpec((rows, block), lambda s, o: (0, s)),
    ]
    args = [order, out_weight, out_weight, g_a, g_b]
    if not first:
        in_specs.append(pl.BlockSpec((feat, rows), lambda s, o: (0, 0)))
        args.append(begin)
    return pl.pallas_call(
        functools.partial(matmul_kernel, first, not first),
        grid_spec=pltpu.PrefetchScalarGridSpec(
            num_scalar_prefetch=1,
            grid=(steps,),
            in_specs=in_specs,
            out_specs=pl.BlockSpec((feat, rows), lambda s, o: (0, 0)),
            scratch_shapes=[pltpu.VMEM((feat, rows), jnp.float32)],
        ),
        out_shape=jax.ShapeDtypeStruct((feat, rows), dtype),
        compiler_params=pltpu.CompilerParams(vmem_limit_bytes=VMEM_LIMIT),
        cost_estimate=pl.CostEstimate(
            flops=4 * feat * rows * cols, bytes_accessed=4 * feat * cols, transcendentals=0
        ),
    )(*args)


def bias_row(live_flags):
    parts = [
        jnp.full((1, TILE), jnp.where(flag, 0.0, -jnp.inf).astype(jnp.float32))
        for flag in live_flags
    ]
    return jnp.concatenate(parts, axis=1)


def query_kernel(pos_ref, mask_ref, q_ref, k_ref, v_ref, kx, vx, kg, vg, ku, vu, kd, vd, d_ref,
                 dq_ref, send_ref):
    pos = pos_ref[0]
    rows = q_ref.shape[0]
    tiles = rows // TILE
    pair_off = 1 - 2 * lax.rem(pos, 2)
    blocks = [
        (k_ref, v_ref, 0), (kx, vx, pair_off), (ku, vu, -2), (kd, vd, 2), (kg, vg, -pair_off)
    ]
    q = q_ref[...]
    shifted = []
    top = None
    for keys, _, off in blocks:
        scores = dot(keys[...], q, NT)
        for b in range(tiles):
            column = (off + SPAN) * tiles + b
            flags = [mask_ref[pos * tiles + a, column] > 0 for a in range(tiles)]
            value = scores[b * TILE:(b + 1) * TILE] * SCALE_LOG2 + bias_row(flags)
            shifted.append(value)
            peak = jnp.max(value, axis=0, keepdims=True)
            top = peak if top is None else jnp.maximum(top, peak)
    weights = []
    totals = None
    for value in shifted:
        weight = jnp.exp2(value - top)
        weights.append(weight)
        part = jnp.sum(weight, axis=0, keepdims=True)
        totals = part if totals is None else totals + part
    out = None
    for n, (_, values, _) in enumerate(blocks):
        w = jnp.concatenate(weights[n * tiles:(n + 1) * tiles], axis=0)
        part = dot(values[...], w.astype(jnp.bfloat16), TN)
        out = part if out is None else out + part
    inverse = 1.0 / totals
    attn_out = (out / totals).astype(jnp.bfloat16).astype(jnp.float32)
    grad = d_ref[...]
    delta = jnp.sum(grad.astype(jnp.float32) * attn_out, axis=0, keepdims=True)
    dq = None
    for n, (keys, values, _) in enumerate(blocks):
        w = jnp.concatenate(weights[n * tiles:(n + 1) * tiles], axis=0)
        dprobs = dot(values[...], grad, NN)
        dscores = (w * inverse * (dprobs - delta)).astype(jnp.bfloat16)
        part = dot(keys[...], dscores, TN)
        dq = part if dq is None else dq + part
    dq_ref[...] = jnp.transpose(dq * SCALE).astype(dq_ref.dtype)
    lse = top + jnp.log2(totals)
    pieces = []
    for stat in (lse, delta):
        for _ in range(3):
            piece = stat.astype(jnp.bfloat16).astype(jnp.float32)
            pieces.append(piece)
            stat = stat - piece
    row = lax.broadcasted_iota(jnp.int32, (STAT_ROWS, rows), 0)
    stats = jnp.zeros((STAT_ROWS, rows), jnp.float32)
    for n, piece in enumerate(pieces):
        stats = jnp.where(row == n, piece, stats)
    send_ref[:HEAD_DIM, :] = grad
    send_ref[HEAD_DIM:, :] = stats.astype(jnp.bfloat16)


def query_side(pos, tile_mask, queries, keys, values, windows, d_out_t):
    rows, feat = queries.shape
    heads = feat // HEAD_DIM
    own = pl.BlockSpec((rows, HEAD_DIM), lambda h, *_: (0, h))
    second = pl.BlockSpec((rows, HEAD_DIM), lambda h, *_: (1, h))
    in_specs = [own, own, own]
    args = [queries, keys, values]
    for window in windows:
        in_specs += [own, second]
        args += [window, window]
    in_specs.append(pl.BlockSpec((HEAD_DIM, rows), lambda h, *_: (h, 0)))
    args.append(d_out_t)
    packed = HEAD_DIM + STAT_ROWS
    return pl.pallas_call(
        query_kernel,
        grid_spec=pltpu.PrefetchScalarGridSpec(
            num_scalar_prefetch=2,
            grid=(heads,),
            in_specs=in_specs,
            out_specs=[own, pl.BlockSpec((packed, rows), lambda h, *_: (h, 0))],
        ),
        out_shape=[
            jax.ShapeDtypeStruct((rows, feat), jnp.bfloat16),
            jax.ShapeDtypeStruct((heads * packed, rows), jnp.bfloat16),
        ],
        compiler_params=pltpu.CompilerParams(vmem_limit_bytes=VMEM_LIMIT),
        cost_estimate=pl.CostEstimate(
            flops=2 * 4 * 5 * rows * rows * feat, bytes_accessed=2 * 15 * rows * feat,
            transcendentals=5 * rows * rows * heads,
        ),
    )(pos, tile_mask, *args)


def key_kernel(offsets, pos_ref, mask_ref, k_ref, v_ref, *rest):
    count = len(offsets)
    pairs = [(rest[2 * n], rest[2 * n + 1]) for n in range(count)]
    dk_ref, dv_ref = rest[2 * count:]
    pos = pos_ref[0]
    rows = k_ref.shape[0]
    tiles = rows // TILE
    total_tiles = mask_ref.shape[0]
    pair_off = 1 - 2 * lax.rem(pos, 2)
    keys, values = k_ref[...], v_ref[...]
    dk = dv = None
    for (q_ref, packed), offset in zip(pairs, offsets):
        off = {"pair": pair_off, "across": -pair_off}.get(offset, offset)
        q = q_ref[...]
        grad = packed[:HEAD_DIM, :]
        stats = packed[HEAD_DIM:, :].astype(jnp.float32)
        lse = stats[0:1] + stats[1:2] + stats[2:3]
        delta = stats[3:4] + stats[4:5] + stats[5:6]
        scores = dot(keys, q, NT)
        probs = []
        for b in range(tiles):
            flags = []
            for a in range(tiles):
                tile = (pos + off) * tiles + a
                inside = (tile >= 0) & (tile < total_tiles)
                column = (SPAN - off) * tiles + b
                flags.append(inside & (mask_ref[jnp.clip(tile, 0, total_tiles - 1), column] > 0))
            shift = bias_row(flags) - lse
            probs.append(jnp.exp2(scores[b * TILE:(b + 1) * TILE] * SCALE_LOG2 + shift))
        probs = jnp.concatenate(probs, axis=0)
        dv_part = dot(probs.astype(jnp.bfloat16), grad, NT)
        dprobs = dot(values, grad, NN)
        dscores = (probs * (dprobs - delta)).astype(jnp.bfloat16)
        dk_part = dot(dscores, q, NN)
        dk = dk_part if dk is None else dk + dk_part
        dv = dv_part if dv is None else dv + dv_part
    dk_ref[...] = (dk * SCALE).astype(dk_ref.dtype)
    dv_ref[...] = dv.astype(dv_ref.dtype)


def key_side(pos, tile_mask, keys, values, sources):
    rows, feat = keys.shape
    heads = feat // HEAD_DIM
    own = pl.BlockSpec((rows, HEAD_DIM), lambda h, *_: (0, h))
    packed = pl.BlockSpec((HEAD_DIM + STAT_ROWS, rows), lambda h, *_: (h, 0))
    in_specs = [own, own]
    args = [keys, values]
    for q, p, _ in sources:
        in_specs += [own, packed]
        args += [q, p]
    return pl.pallas_call(
        functools.partial(key_kernel, [offset for _, _, offset in sources]),
        grid_spec=pltpu.PrefetchScalarGridSpec(
            num_scalar_prefetch=2,
            grid=(heads,),
            in_specs=in_specs,
            out_specs=[own, own],
        ),
        out_shape=[jax.ShapeDtypeStruct((rows, feat), jnp.bfloat16)] * 2,
        compiler_params=pltpu.CompilerParams(vmem_limit_bytes=VMEM_LIMIT),
        cost_estimate=pl.CostEstimate(
            flops=2 * 4 * 5 * rows * rows * feat, bytes_accessed=2 * 14 * rows * feat,
            transcendentals=5 * rows * rows * heads,
        ),
    )(pos, tile_mask, *args)


def local(queries, keys, values, out_weight, reward_grad, tile_mask):
    ctx = lax.axis_index("ctx").astype(jnp.int32)
    head = lax.axis_index("head").astype(jnp.int32)
    pos = ctx.reshape(1)

    far = send(reward_grad, lambda c, h: (c, h ^ 2))
    near = send(reward_grad, lambda c, h: (c, h ^ 1))
    kv = jnp.concatenate([keys, values], axis=0)
    kv_x = send(kv, pair_up)
    kv_u = send(kv, upward)
    kv_d = send(kv, downward)
    begun = partial_out(
        jnp.stack([head, head ^ 1]), out_weight, reward_grad, near, None, jnp.float32
    )

    def second_step(x, u, d):
        held = jnp.where(ctx % 2 == 1, u, d)
        return send(jnp.where(head % 2 == 1, held, x), forward)

    kv_g = second_step(kv_x, kv_u, kv_d)
    far_near = send(far, lambda c, h: (c, h ^ 1))
    queries_late = after(queries, kv_x, kv_u, kv_d)
    q_x = send(queries_late, pair_up)
    q_u = send(queries_late, upward)
    q_d = send(queries_late, downward)
    d_out_t = partial_out(
        jnp.stack([head ^ 2, head ^ 3]), out_weight, far, far_near, begun, jnp.bfloat16
    )
    grad_queries, packed = query_side(
        pos, tile_mask, queries, keys, values, [kv_x, kv_g, kv_u, kv_d], d_out_t
    )
    q_g = second_step(q_x, q_u, q_d)
    p_g = send(packed, across)
    p_x = send(packed, pair_up)
    p_u = send(packed, upward)
    p_d = send(packed, downward)
    grad_keys, grad_values = key_side(
        pos,
        tile_mask,
        keys,
        values,
        [
            (queries, packed, 0),
            (q_x, p_x, "pair"),
            (q_u, p_u, -2),
            (q_d, p_d, 2),
            (q_g, p_g, "across"),
        ],
    )
    return (grad_queries, grad_keys, grad_values)


def solution(mesh):
    placed = (
        P("ctx", "head"),
        P("ctx", "head"),
        P("ctx", "head"),
        P("head", None),
        P("ctx", "head"),
        P(),
    )
    return jax.shard_map(
        local,
        mesh=mesh,
        in_specs=placed,
        out_specs=(P("ctx", "head"), P("ctx", "head"), P("ctx", "head")),
        check_vma=False,
    )
```

```python
import functools
import math

import jax
import jax.numpy as jnp
from jax import lax
from jax.experimental import pallas as pl
from jax.experimental.pallas import tpu as pltpu
from jax.sharding import PartitionSpec as P

HEAD_DIM = 128
TILE = 128
SPAN = 2
STAT_ROWS = 16
SCALE = 1.0 / math.sqrt(HEAD_DIM)
SCALE_LOG2 = SCALE * math.log2(math.e)
BOTH = ("ctx", "head")
NT = (((1,), (1,)), ((), ()))
TN = (((0,), (0,)), ((), ()))
NN = (((1,), (0,)), ((), ()))
VMEM_LIMIT = 24 * 1024 * 1024
VMEM = pl.BlockSpec(memory_space=pltpu.VMEM)
SMEM = pl.BlockSpec(memory_space=pltpu.SMEM)


def dot(a, b, dims):
    return lax.dot_general(a, b, dims, preferred_element_type=jnp.float32)


def kernel_call(kernel, out_shape, operands, flops, transcendentals=0):
    moved = sum(x.size * x.dtype.itemsize for x in operands)
    return pl.pallas_call(
        kernel,
        in_specs=[SMEM if x.dtype == jnp.int32 else VMEM for x in operands],
        out_specs=jax.tree.map(lambda _: VMEM, out_shape),
        out_shape=out_shape,
        compiler_params=pltpu.CompilerParams(vmem_limit_bytes=VMEM_LIMIT),
        cost_estimate=pl.CostEstimate(
            flops=flops, bytes_accessed=moved, transcendentals=transcendentals
        ),
    )(*operands)


def send(array, rule):
    n_ctx, n_head = lax.axis_size("ctx"), lax.axis_size("head")
    pairs = []
    for c in range(n_ctx):
        for h in range(n_head):
            to = rule(c, h)
            if 0 <= to[0] < n_ctx:
                pairs.append((c * n_head + h, to[0] * n_head + to[1]))
    return lax.ppermute(array, BOTH, pairs)


def in_pair(c, h):
    return (c ^ 1, h)


def even_chain(c, h):
    return (c ^ 2, h)


def odd_chain(c, h):
    return (c + 2, h) if c & 2 else (c - 2, h)


def across(c, h):
    return (c + 1, h) if c & 1 else (c - 1, h)


def forward(c, h):
    if h & 1:
        return (c ^ 1, h)
    return (c - 2, h) if c & 1 else (c + 2, h)


def offsets(pos):
    pair = 1 - 2 * lax.rem(pos, 2)
    chain = 2 - 4 * lax.rem(pos // 2, 2)
    return pair, chain, -chain, -pair


def after(value, *others):
    return lax.optimization_barrier((value,) + others)[0]


def project_kernel(order_ref, w_ref, g_a, g_b, *rest):
    cols = g_a.shape[1]
    total = None
    for n, g_ref in enumerate((g_a, g_b)):
        start = pl.multiple_of(order_ref[n] * cols, cols)
        part = dot(w_ref[:, pl.ds(start, cols)], g_ref[...], NT)
        total = part if total is None else total + part
    out_ref = rest[-1]
    if len(rest) == 2:
        total = total + rest[0][...]
    out_ref[...] = total.astype(out_ref.dtype)


def project(order, out_weight, g_a, g_b, begun=None):
    rows, cols = g_a.shape
    feat = out_weight.shape[0]
    operands = [order, out_weight, g_a, g_b] + ([] if begun is None else [begun])
    dtype = jnp.float32 if begun is None else jnp.bfloat16
    return kernel_call(
        project_kernel,
        jax.ShapeDtypeStruct((feat, rows), dtype),
        operands,
        4 * rows * cols * feat,
    )


def bias_row(live_flags):
    parts = [
        jnp.full((1, TILE), jnp.where(flag, 0.0, -jnp.inf).astype(jnp.float32))
        for flag in live_flags
    ]
    return jnp.concatenate(parts, axis=1)


def over_keys(reduce, values):
    return reduce(values.reshape(TILE // 8, 8, values.shape[1]), axis=0)


def query_kernel(pos_ref, mask_ref, q_ref, k_ref, v_ref, w_x, w_a, w_b, w_g, d_ref,
                 dq_ref, packed_ref, stats_ref):
    pos = pos_ref[0]
    rows, feat = q_ref.shape
    tiles, heads = rows // TILE, feat // HEAD_DIM
    windows = [None, w_x, w_a, w_b, w_g]
    biases = []
    for off in (0,) + offsets(pos):
        for b in range(tiles):
            column = (off + SPAN) * tiles + b
            flags = [mask_ref[pos * tiles + a, column] > 0 for a in range(tiles)]
            biases.append(bias_row(flags))

    def keys_of(n, cols):
        return k_ref[:, cols] if windows[n] is None else windows[n][:rows, cols]

    def values_of(n, cols):
        return v_ref[:, cols] if windows[n] is None else windows[n][rows:, cols]

    def score(head):
        cols = slice(head * HEAD_DIM, (head + 1) * HEAD_DIM)
        q = q_ref[:, cols]
        return [dot(keys_of(n, cols), q, NT) for n in range(len(windows))]

    def finish(head, scores):
        cols = slice(head * HEAD_DIM, (head + 1) * HEAD_DIM)
        shifted = []
        top = None
        for n, block in enumerate(scores):
            for b in range(tiles):
                value = block[b * TILE:(b + 1) * TILE] * SCALE_LOG2 + biases[n * tiles + b]
                shifted.append(value)
                peak = over_keys(jnp.max, value)
                top = peak if top is None else jnp.maximum(top, peak)
        top = jnp.max(top, axis=0, keepdims=True)
        weights = []
        totals = out = None
        for n in range(len(windows)):
            parts = []
            for b in range(tiles):
                weight = jnp.exp2(shifted[n * tiles + b] - top)
                parts.append(weight)
                part = over_keys(jnp.sum, weight)
                totals = part if totals is None else totals + part
            weights.append(jnp.concatenate(parts, axis=0))
            part = dot(values_of(n, cols), weights[-1].astype(jnp.bfloat16), TN)
            out = part if out is None else out + part
        totals = jnp.sum(totals, axis=0, keepdims=True)
        inverse = 1.0 / totals
        attn_out = (out / totals).astype(jnp.bfloat16).astype(jnp.float32)
        grad = d_ref[cols, :]
        delta = jnp.sum(grad.astype(jnp.float32) * attn_out, axis=0, keepdims=True)
        dq = None
        for n in range(len(windows)):
            dprobs = dot(values_of(n, cols), grad, NN)
            dscores = (weights[n] * ((dprobs - delta) * inverse)).astype(jnp.bfloat16)
            part = dot(keys_of(n, cols), dscores, TN)
            dq = part if dq is None else dq + part
        dq_ref[:, cols] = jnp.transpose(dq * SCALE).astype(dq_ref.dtype)
        stats = jnp.zeros((STAT_ROWS, rows), jnp.float32)
        row = lax.broadcasted_iota(jnp.int32, (STAT_ROWS, rows), 0)
        at = 0
        for stat in (top + jnp.log2(totals), delta):
            for _ in range(3):
                piece = stat.astype(jnp.bfloat16).astype(jnp.float32)
                stats = jnp.where(row == at, piece, stats)
                stat = stat - piece
                at += 1
        stats = stats.astype(jnp.bfloat16)
        packed_ref[cols, :] = grad
        packed_ref[feat + head * STAT_ROWS:feat + (head + 1) * STAT_ROWS, :] = stats
        stats_ref[head * STAT_ROWS:(head + 1) * STAT_ROWS, :] = stats

    ahead = score(0)
    for head in range(heads):
        scores = ahead
        if head + 1 < heads:
            ahead = score(head + 1)
        finish(head, scores)


def query_side(pos, tile_mask, queries, keys, values, windows, d_out_t):
    rows, feat = queries.shape
    stat_rows = feat // HEAD_DIM * STAT_ROWS
    return kernel_call(
        query_kernel,
        [
            jax.ShapeDtypeStruct((rows, feat), jnp.bfloat16),
            jax.ShapeDtypeStruct((feat + stat_rows, rows), jnp.bfloat16),
            jax.ShapeDtypeStruct((stat_rows, rows), jnp.bfloat16),
        ],
        [pos, tile_mask, queries, keys, values, *windows, d_out_t],
        40 * rows * rows * feat,
        5 * rows * rows * feat // HEAD_DIM,
    )


def key_kernel(which, stats_at, final, pos_ref, mask_ref, k_ref, v_ref, *rest):
    count = len(which)
    sources = [rest[3 * n:3 * n + 3] for n in range(count)]
    rest = rest[3 * count:]
    begun, (dk_ref, dv_ref) = (rest[:2], rest[2:]) if final else (None, rest)
    pos = pos_ref[0]
    rows, feat = k_ref.shape
    tiles, heads = rows // TILE, feat // HEAD_DIM
    total_tiles = mask_ref.shape[0]
    offs = (0,) + offsets(pos)
    biases = []
    for n in which:
        for b in range(tiles):
            flags = []
            for a in range(tiles):
                tile = (pos + offs[n]) * tiles + a
                inside = (tile >= 0) & (tile < total_tiles)
                column = (SPAN - offs[n]) * tiles + b
                flags.append(inside & (mask_ref[jnp.clip(tile, 0, total_tiles - 1), column] > 0))
            biases.append(bias_row(flags))

    def columns(head):
        return slice(head * HEAD_DIM, (head + 1) * HEAD_DIM)

    def products(head, n):
        cols = columns(head)
        q_ref, d_ref, _ = sources[n]
        return dot(k_ref[:, cols], q_ref[:, cols], NT), dot(v_ref[:, cols], d_ref[cols, :], NN)

    def finish(head, n, scores, dprobs):
        cols = columns(head)
        q_ref, d_ref, s_ref = sources[n]
        at = stats_at[n] + head * STAT_ROWS
        stats = s_ref[at:at + STAT_ROWS, :].astype(jnp.float32)
        lse = stats[0:1] + stats[1:2] + stats[2:3]
        delta = stats[3:4] + stats[4:5] + stats[5:6]
        probs = jnp.concatenate(
            [
                jnp.exp2(
                    scores[b * TILE:(b + 1) * TILE] * SCALE_LOG2 + (biases[n * tiles + b] - lse)
                )
                for b in range(tiles)
            ],
            axis=0,
        )
        dv = dot(probs.astype(jnp.bfloat16), d_ref[cols, :], NT)
        dscores = (probs * (dprobs - delta)).astype(jnp.bfloat16)
        return dot(dscores, q_ref[:, cols], NN), dv

    steps = [(head, n) for head in range(heads) for n in range(count)]
    ahead = products(*steps[0])
    for at, (head, n) in enumerate(steps):
        now = ahead
        if at + 1 < len(steps):
            ahead = products(*steps[at + 1])
        dk_part, dv_part = finish(head, n, *now)
        cols = columns(head)
        if n == 0:
            dk, dv = dk_part, dv_part
            if final:
                dk, dv = dk + begun[0][:, cols], dv + begun[1][:, cols]
        else:
            dk, dv = dk + dk_part, dv + dv_part
        if n == count - 1:
            dk_ref[:, cols] = (dk * SCALE if final else dk).astype(dk_ref.dtype)
            dv_ref[:, cols] = dv.astype(dv_ref.dtype)


def key_side(pos, tile_mask, keys, values, sources, begun=()):
    rows, feat = keys.shape
    operands = [pos, tile_mask, keys, values]
    for _, q, d, s in sources:
        operands += [q, d, s]
    operands += begun
    which = [n for n, _, _, _ in sources]
    stats_at = [s.shape[0] - feat // HEAD_DIM * STAT_ROWS for _, _, _, s in sources]
    dtype = jnp.bfloat16 if begun else jnp.float32
    return kernel_call(
        functools.partial(key_kernel, which, stats_at, bool(begun)),
        [jax.ShapeDtypeStruct((rows, feat), dtype)] * 2,
        operands,
        8 * len(which) * rows * rows * feat,
        len(which) * rows * rows * feat // HEAD_DIM,
    )


def local(queries, keys, values, out_weight, reward_grad, tile_mask):
    ctx = lax.axis_index("ctx").astype(jnp.int32)
    head = lax.axis_index("head").astype(jnp.int32)
    pos = ctx.reshape(1)

    def second_step(x, a, b):
        a_is_held = (ctx % 2 == 0) == (ctx // 2 % 2 == 0)
        return jnp.where(head % 2 == 1, jnp.where(a_is_held, a, b), x)

    far = send(reward_grad, lambda c, h: (c, h ^ 2))
    kv = jnp.concatenate([keys, values], axis=0)
    kv_a = send(kv, even_chain)
    kv_b = send(kv, odd_chain)
    kv_x = send(kv, in_pair)
    near = send(reward_grad, lambda c, h: (c, h ^ 1))
    begun = project(jnp.stack([head, head ^ 1]), out_weight, reward_grad, near)
    far_near = send(far, lambda c, h: (c, h ^ 1))
    late_queries = after(queries, begun, far)
    q_a = send(late_queries, even_chain)
    q_b = send(late_queries, odd_chain)
    q_x = send(late_queries, in_pair)
    kv_g = send(second_step(kv_x, kv_a, kv_b), forward)
    d_out_t = project(jnp.stack([head ^ 2, head ^ 3]), out_weight, far, far_near, begun)
    d_g = send(d_out_t, across)
    q_g = send(second_step(q_x, q_a, q_b), forward)
    grad_queries, packed, stats = query_side(
        pos, tile_mask, queries, keys, values, [kv_x, kv_a, kv_b, kv_g], d_out_t
    )
    p_a = send(packed, even_chain)
    p_b = send(packed, odd_chain)
    p_x = send(packed, in_pair)
    s_g = send(stats, across)
    begun_keys = key_side(
        pos,
        tile_mask,
        keys,
        values,
        [(0, queries, packed, packed), (4, q_g, d_g, s_g)],
    )
    grad_keys, grad_values = key_side(
        pos,
        tile_mask,
        keys,
        values,
        [(1, q_x, p_x, p_x), (2, q_a, p_a, p_a), (3, q_b, p_b, p_b)],
        begun_keys,
    )
    return (grad_queries, grad_keys, grad_values)


def solution(mesh):
    placed = (
        P("ctx", "head"),
        P("ctx", "head"),
        P("ctx", "head"),
        P("head", None),
        P("ctx", "head"),
        P(),
    )
    return jax.shard_map(
        local,
        mesh=mesh,
        in_specs=placed,
        out_specs=(P("ctx", "head"), P("ctx", "head"), P("ctx", "head")),
        check_vma=False,
    )
```

```python
import functools
import math

import jax
import jax.numpy as jnp
from jax import lax
from jax.experimental import pallas as pl
from jax.experimental.pallas import tpu as pltpu
from jax.sharding import PartitionSpec as P

HEAD_DIM = 128
TILE = 128
SPAN = 2
STAT_ROWS = 16
SCALE = 1.0 / math.sqrt(HEAD_DIM)
SCALE_LOG2 = SCALE * math.log2(math.e)
BOTH = ("ctx", "head")
NT = (((1,), (1,)), ((), ()))
TN = (((0,), (0,)), ((), ()))
NN = (((1,), (0,)), ((), ()))
VMEM_LIMIT = 16 * 1024 * 1024
VMEM_ALONE = 32 * 1024 * 1024
VMEM = pl.BlockSpec(memory_space=pltpu.VMEM)
SMEM = pl.BlockSpec(memory_space=pltpu.SMEM)
ANY = pl.BlockSpec(memory_space=pl.ANY)


def dot(a, b, dims):
    return lax.dot_general(a, b, dims, preferred_element_type=jnp.float32)


def kernel_call(kernel, out_shape, operands, flops, transcendentals=0):
    moved = sum(x.size * x.dtype.itemsize for x in operands)
    return pl.pallas_call(
        kernel,
        in_specs=[SMEM if x.dtype == jnp.int32 else VMEM for x in operands],
        out_specs=jax.tree.map(lambda _: VMEM, out_shape),
        out_shape=out_shape,
        compiler_params=pltpu.CompilerParams(vmem_limit_bytes=VMEM_LIMIT),
        cost_estimate=pl.CostEstimate(
            flops=flops, bytes_accessed=moved, transcendentals=transcendentals
        ),
    )(*operands)


def send(array, rule):
    n_ctx, n_head = lax.axis_size("ctx"), lax.axis_size("head")
    pairs = []
    for c in range(n_ctx):
        for h in range(n_head):
            to = rule(c, h)
            if 0 <= to[0] < n_ctx:
                pairs.append((c * n_head + h, to[0] * n_head + to[1]))
    return lax.ppermute(array, BOTH, pairs)


def in_pair(c, h):
    return (c ^ 1, h)


def even_chain(c, h):
    return (c ^ 2, h)


def odd_chain(c, h):
    return (c + 2, h) if c & 2 else (c - 2, h)


def across(c, h):
    return (c + 1, h) if c & 1 else (c - 1, h)


def forward(c, h):
    if h & 1:
        return (c ^ 1, h)
    return (c - 2, h) if c & 1 else (c + 2, h)


def offsets(pos):
    pair = 1 - 2 * lax.rem(pos, 2)
    chain = 2 - 4 * lax.rem(pos // 2, 2)
    return pair, chain, -chain, -pair


def after(value, *others):
    return lax.optimization_barrier((value,) + others)[0]


def pack_kernel(k_ref, v_ref, out_ref, sems):
    rows = k_ref.shape[0]
    copies = [
        pltpu.make_async_copy(k_ref, out_ref.at[:rows], sems.at[0]),
        pltpu.make_async_copy(v_ref, out_ref.at[rows:], sems.at[1]),
    ]
    for copy in copies:
        copy.start()
    for copy in copies:
        copy.wait()


def pack(keys, values):
    rows, feat = keys.shape
    return pl.pallas_call(
        pack_kernel,
        in_specs=[ANY] * 2,
        out_specs=VMEM,
        out_shape=jax.ShapeDtypeStruct((2 * rows, feat), keys.dtype),
        scratch_shapes=[pltpu.SemaphoreType.DMA((2,))],
        compiler_params=pltpu.CompilerParams(vmem_limit_bytes=VMEM_LIMIT),
        cost_estimate=pl.CostEstimate(
            flops=0, bytes_accessed=60_000_000, transcendentals=0
        ),
    )(keys, values)


def begin_kernel(order_ref, w_ref, g_a, g_b, out_ref, kept_ref, used, sems):
    cols = g_a.shape[1]
    copies = []
    for n in range(4):
        start = pl.multiple_of(order_ref[n] * cols, cols)
        to = used.at[n] if n < 2 else kept_ref.at[:, (n - 2) * cols:(n - 1) * cols]
        copies.append(pltpu.make_async_copy(w_ref.at[:, pl.ds(start, cols)], to, sems.at[n]))
        copies[-1].start()
    copies[0].wait()
    total = dot(used[0], g_a[...], NT)
    copies[1].wait()
    out_ref[...] = total + dot(used[1], g_b[...], NT)
    copies[2].wait()
    copies[3].wait()


def begin_project(order, out_weight, g_a, g_b):
    rows, cols = g_a.shape
    feat = out_weight.shape[0]
    return pl.pallas_call(
        begin_kernel,
        in_specs=[SMEM, ANY, VMEM, VMEM],
        out_specs=[VMEM, VMEM],
        out_shape=[
            jax.ShapeDtypeStruct((feat, rows), jnp.float32),
            jax.ShapeDtypeStruct((feat, 2 * cols), out_weight.dtype),
        ],
        scratch_shapes=[
            pltpu.VMEM((2, feat, cols), out_weight.dtype),
            pltpu.SemaphoreType.DMA((4,)),
        ],
        compiler_params=pltpu.CompilerParams(vmem_limit_bytes=VMEM_ALONE),
        cost_estimate=pl.CostEstimate(
            flops=4 * rows * cols * feat, bytes_accessed=8 * feat * cols, transcendentals=0
        ),
    )(order, out_weight, g_a, g_b)


def end_kernel(w_ref, g_a, g_b, begun, out_ref):
    cols = g_a.shape[1]
    total = begun[...] + dot(w_ref[:, :cols], g_a[...], NT)
    out_ref[...] = (total + dot(w_ref[:, cols:], g_b[...], NT)).astype(out_ref.dtype)


def end_project(weight, g_a, g_b, begun):
    rows, cols = g_a.shape
    feat = weight.shape[0]
    return kernel_call(
        end_kernel,
        jax.ShapeDtypeStruct((feat, rows), jnp.bfloat16),
        [weight, g_a, g_b, begun],
        4 * rows * cols * feat,
    )


def columns(head):
    return slice(head * HEAD_DIM, (head + 1) * HEAD_DIM)


def stat_slice(head, start=0):
    return slice(start + head * STAT_ROWS, start + (head + 1) * STAT_ROWS)


def bias_row(live_flags):
    parts = [
        jnp.full((1, TILE), jnp.where(flag, 0.0, -jnp.inf).astype(jnp.float32))
        for flag in live_flags
    ]
    return jnp.concatenate(parts, axis=1)


def window_bias(mask_ref, pos, tiles, which):
    offs = (0,) + offsets(pos)
    return [
        [
            bias_row(
                [
                    mask_ref[pos * tiles + a, (offs[n] + SPAN) * tiles + b] > 0
                    for a in range(tiles)
                ]
            )
            for b in range(tiles)
        ]
        for n in which
    ]


def source_bias(mask_ref, pos, tiles, which):
    total_tiles = mask_ref.shape[0]
    offs = (0,) + offsets(pos)
    rows = []
    for n in which:
        rows.append([])
        for b in range(tiles):
            flags = []
            for a in range(tiles):
                tile = (pos + offs[n]) * tiles + a
                inside = (tile >= 0) & (tile < total_tiles)
                column = (SPAN - offs[n]) * tiles + b
                flags.append(inside & (mask_ref[jnp.clip(tile, 0, total_tiles - 1), column] > 0))
            rows[-1].append(bias_row(flags))
    return rows


def over_keys(reduce, values):
    return reduce(values.reshape(TILE // 8, 8, values.shape[1]), axis=0)


def softmax_part(scores, biases):
    shifted = []
    top = None
    for block, rows in zip(scores, biases):
        shifted.append([])
        for b, row in enumerate(rows):
            value = block[b * TILE:(b + 1) * TILE] * SCALE_LOG2 + row
            shifted[-1].append(value)
            peak = over_keys(jnp.max, value)
            top = peak if top is None else jnp.maximum(top, peak)
    return shifted, jnp.max(top, axis=0, keepdims=True)


def weighted_values(shifted, top, values_of):
    totals = out = None
    for n, parts in enumerate(shifted):
        weights = []
        for value in parts:
            weight = jnp.exp2(value - top)
            weights.append(weight)
            part = over_keys(jnp.sum, weight)
            totals = part if totals is None else totals + part
        part = dot(values_of(n), jnp.concatenate(weights, axis=0).astype(jnp.bfloat16), TN)
        out = part if out is None else out + part
    return jnp.sum(totals, axis=0, keepdims=True), out


def in_order(steps, ahead_of, finish):
    ahead = ahead_of(*steps[0])
    for at, step in enumerate(steps):
        now = ahead
        if at + 1 < len(steps):
            ahead = ahead_of(*steps[at + 1])
        finish(*step, now)


def forward_kernel(which, pos_ref, mask_ref, q_ref, *rest):
    windows, (out_ref, run_ref) = rest[:len(which)], rest[len(which):]
    pos = pos_ref[0]
    rows, feat = q_ref.shape
    biases = window_bias(mask_ref, pos, rows // TILE, which)

    def scores_of(head):
        cols = columns(head)
        q = q_ref[:, cols]
        return [dot(w[:rows, cols], q, NT) for w in windows]

    def finish(head, scores):
        cols = columns(head)

        def values_of(n):
            return windows[n][rows:, cols]

        shifted, top = softmax_part(scores, biases)
        totals, out = weighted_values(shifted, top, values_of)
        out_ref[cols, :] = out
        at = head * STAT_ROWS
        run_ref[at:at + 8, :] = jnp.broadcast_to(top, (8, rows))
        run_ref[at + 8:at + 16, :] = jnp.broadcast_to(totals, (8, rows))

    in_order([(head,) for head in range(feat // HEAD_DIM)], scores_of, finish)


def forward_part(pos, tile_mask, queries, which, windows):
    rows, feat = queries.shape
    heads = feat // HEAD_DIM
    return kernel_call(
        functools.partial(forward_kernel, which),
        [
            jax.ShapeDtypeStruct((feat, rows), jnp.float32),
            jax.ShapeDtypeStruct((heads * STAT_ROWS, rows), jnp.float32),
        ],
        [pos, tile_mask, queries, *windows],
        4 * len(which) * rows * rows * feat,
        len(which) * rows * rows * heads,
    )


def statistics_kernel(
    which, pos_ref, mask_ref, q_ref, w_ref, out_in, run_in, d_ref, stats_ref, packed_ref
):
    pos = pos_ref[0]
    rows, feat = q_ref.shape
    biases = window_bias(mask_ref, pos, rows // TILE, [which])

    def scores_of(head):
        cols = columns(head)
        return [dot(w_ref[:rows, cols], q_ref[:, cols], NT)]

    def finish(head, scores):
        cols = columns(head)

        def values_of(n):
            return w_ref[rows:, cols]

        at = head * STAT_ROWS
        top_before, totals_before = run_in[at:at + 1, :], run_in[at + 8:at + 9, :]
        shifted, top = softmax_part(scores, biases)
        top = jnp.maximum(top, top_before)
        totals, out = weighted_values(shifted, top, values_of)
        shrink = jnp.exp2(top_before - top)
        totals = totals + totals_before * shrink
        out = out + out_in[cols, :] * shrink
        attn_out = (out / totals).astype(jnp.bfloat16).astype(jnp.float32)
        delta = jnp.sum(d_ref[cols, :].astype(jnp.float32) * attn_out, axis=0, keepdims=True)
        row = lax.broadcasted_iota(jnp.int32, (STAT_ROWS, rows), 0)
        stats = jnp.zeros((STAT_ROWS, rows), jnp.float32)
        place = 0
        for stat in (top + jnp.log2(totals), delta):
            for _ in range(3):
                piece = stat.astype(jnp.bfloat16).astype(jnp.float32)
                stats = jnp.where(row == place, piece, stats)
                stat = stat - piece
                place += 1
        stats_ref[stat_slice(head), :] = stats.astype(jnp.bfloat16)
        packed_ref[cols, :] = d_ref[cols, :]
        packed_ref[stat_slice(head, feat), :] = stats.astype(jnp.bfloat16)

    in_order([(head,) for head in range(feat // HEAD_DIM)], scores_of, finish)


def statistics(pos, tile_mask, queries, which, window, out, run, d_out_t):
    rows, feat = queries.shape
    heads = feat // HEAD_DIM
    return kernel_call(
        functools.partial(statistics_kernel, which),
        [
            jax.ShapeDtypeStruct((heads * STAT_ROWS, rows), jnp.bfloat16),
            jax.ShapeDtypeStruct((feat + heads * STAT_ROWS, rows), jnp.bfloat16),
        ],
        [pos, tile_mask, queries, window, out, run, d_out_t],
        4 * rows * rows * feat,
        rows * rows * heads,
    )


def block_grads(scores, dprobs, bias_rows, stats):
    stats = stats.astype(jnp.float32)
    lse = stats[0:1] + stats[1:2] + stats[2:3]
    delta = stats[3:4] + stats[4:5] + stats[5:6]
    probs = jnp.concatenate(
        [
            jnp.exp2(scores[b * TILE:(b + 1) * TILE] * SCALE_LOG2 + (row - lse))
            for b, row in enumerate(bias_rows)
        ],
        axis=0,
    )
    dscores = probs * (dprobs - delta)
    return probs.astype(jnp.bfloat16), dscores.astype(jnp.bfloat16)


def query_kernel(which, pos_ref, mask_ref, q_ref, *rest):
    count = len(which)
    windows = rest[:count]
    d_ref, s_ref, dq_ref, dk_ref, dv_ref = rest[count:]
    rows, feat = q_ref.shape
    biases = window_bias(mask_ref, pos_ref[0], rows // TILE, which)
    sums = [None]

    def keys_of(n, cols):
        return windows[n][:rows, cols]

    def values_of(n, cols):
        return windows[n][rows:, cols]

    def products(head, n):
        cols = columns(head)
        return (
            dot(keys_of(n, cols), q_ref[:, cols], NT),
            dot(values_of(n, cols), d_ref[cols, :], NN),
        )

    def finish(head, n, now):
        cols = columns(head)
        probs, dscores = block_grads(*now, biases[n], s_ref[stat_slice(head), :])
        part = dot(keys_of(n, cols), dscores, TN)
        if n == 0:
            sums[0] = part
            dk_ref[:, cols] = dot(dscores, q_ref[:, cols], NN)
            dv_ref[:, cols] = dot(probs, d_ref[cols, :], NT)
        else:
            sums[0] = sums[0] + part
        if n == count - 1:
            dq_ref[:, cols] = jnp.transpose(sums[0] * SCALE).astype(dq_ref.dtype)

    steps = [(head, n) for head in range(feat // HEAD_DIM) for n in range(count)]
    in_order(steps, products, finish)


def query_side(pos, tile_mask, queries, which, windows, d_out_t, stats):
    rows, feat = queries.shape
    total = jax.ShapeDtypeStruct((rows, feat), jnp.float32)
    return kernel_call(
        functools.partial(query_kernel, which),
        [jax.ShapeDtypeStruct((rows, feat), jnp.bfloat16), total, total],
        [pos, tile_mask, queries, *windows, d_out_t, stats],
        34 * rows * rows * feat,
        5 * rows * rows * feat // HEAD_DIM,
    )


def key_kernel(which, final, pos_ref, mask_ref, kv_ref, *rest):
    count = len(which)
    sources = [rest[3 * n:3 * n + 3] for n in range(count)]
    dk_in, dv_in, dk_ref, dv_ref = rest[3 * count:]
    rows, feat = dk_in.shape
    biases = source_bias(mask_ref, pos_ref[0], rows // TILE, which)
    sums = [None, None]

    def products(head, n):
        cols = columns(head)
        q_ref, d_ref, _ = sources[n]
        return (
            dot(kv_ref[:rows, cols], q_ref[:, cols], NT),
            dot(kv_ref[rows:, cols], d_ref[cols, :], NN),
        )

    def finish(head, n, now):
        cols = columns(head)
        q_ref, d_ref, s_ref = sources[n]
        start = feat if s_ref.shape[0] > feat else 0
        probs, dscores = block_grads(*now, biases[n], s_ref[stat_slice(head, start), :])
        before = (dk_in[:, cols], dv_in[:, cols]) if n == 0 else sums
        sums[:] = [
            before[0] + dot(dscores, q_ref[:, cols], NN),
            before[1] + dot(probs, d_ref[cols, :], NT),
        ]
        if n == count - 1:
            dk, dv = sums
            dk_ref[:, cols] = (dk * SCALE if final else dk).astype(dk_ref.dtype)
            dv_ref[:, cols] = dv.astype(dv_ref.dtype)

    steps = [(head, n) for head in range(feat // HEAD_DIM) for n in range(count)]
    in_order(steps, products, finish)


def key_side(pos, tile_mask, kv, sources, begun, final):
    rows, feat = begun[0].shape
    operands = [pos, tile_mask, kv]
    for _, q, d, s in sources:
        operands += [q, d, s]
    which = [source[0] for source in sources]
    dtype = jnp.bfloat16 if final else jnp.float32
    return kernel_call(
        functools.partial(key_kernel, which, final),
        [jax.ShapeDtypeStruct((rows, feat), dtype)] * 2,
        operands + list(begun),
        8 * len(which) * rows * rows * feat,
        len(which) * rows * rows * feat // HEAD_DIM,
    )


def local(queries, keys, values, out_weight, reward_grad, tile_mask):
    ctx = lax.axis_index("ctx").astype(jnp.int32)
    head = lax.axis_index("head").astype(jnp.int32)
    pos = ctx.reshape(1)

    def second_step(x, a, b):
        a_is_held = (ctx % 2 == 0) == (ctx // 2 % 2 == 0)
        return jnp.where(head % 2 == 1, jnp.where(a_is_held, a, b), x)

    far = send(reward_grad, lambda c, h: (c, h ^ 2))
    kv = pack(keys, values)
    kv_b = send(kv, odd_chain)
    kv_a = send(kv, even_chain)
    kv_x = send(kv, in_pair)
    near = send(after(reward_grad, kv), lambda c, h: (c, h ^ 1))
    order = jnp.stack([head, head ^ 1, head ^ 2, head ^ 3])
    begun, kept = begin_project(order, out_weight, reward_grad, near)
    far = after(far, begun)
    far_near = send(far, lambda c, h: (c, h ^ 1))
    kv_g = send(second_step(kv_x, kv_a, kv_b), forward)
    d_out_t = end_project(kept, far, far_near, begun)
    out, run = forward_part(
        pos, tile_mask, after(queries, d_out_t), [0, 1, 2, 3], [kv, kv_x, kv_a, kv_b]
    )
    late_queries = after(queries, out)
    q_b = send(late_queries, odd_chain)
    q_a = send(late_queries, even_chain)
    q_x = send(late_queries, in_pair)
    stats, packed = statistics(pos, tile_mask, queries, 4, kv_g, out, run, d_out_t)
    p_b = send(packed, odd_chain)
    p_a = send(packed, even_chain)
    p_x = send(packed, in_pair)
    q_g = send(second_step(q_x, q_a, q_b), forward)
    grad_queries, *begun_keys = query_side(
        pos, tile_mask, queries, [0, 1, 2, 3, 4], [kv, kv_x, kv_a, kv_b, kv_g], d_out_t, stats
    )
    p_g = send(second_step(*after((p_x, p_a, p_b), grad_queries)), forward)
    begun_keys = key_side(
        pos,
        tile_mask,
        kv,
        [(1, q_x, p_x, p_x), (2, q_a, p_a, p_a), (3, q_b, p_b, p_b)],
        begun_keys,
        False,
    )
    grad_keys, grad_values = key_side(
        pos, tile_mask, kv, [(4, q_g, p_g, p_g)], begun_keys, True
    )
    return (grad_queries, grad_keys, grad_values)


def solution(mesh):
    placed = (
        P("ctx", "head"),
        P("ctx", "head"),
        P("ctx", "head"),
        P("head", None),
        P("ctx", "head"),
        P(),
    )
    return jax.shard_map(
        local,
        mesh=mesh,
        in_specs=placed,
        out_specs=(P("ctx", "head"), P("ctx", "head"), P("ctx", "head")),
        check_vma=False,
    )
```

```python
import functools
import math

import jax
import jax.numpy as jnp
from jax import lax
from jax.experimental import pallas as pl
from jax.experimental.pallas import tpu as pltpu
from jax.sharding import PartitionSpec as P

HEAD_DIM = 128
TILE = 128
SPAN = 2
RUN_ROWS = 16
STATS = 6
STAT_TILE = 16
SCALE = 1.0 / math.sqrt(HEAD_DIM)
SCALE_LOG2 = SCALE * math.log2(math.e)
BOTH = ("ctx", "head")
NT = (((1,), (1,)), ((), ()))
TN = (((0,), (0,)), ((), ()))
NN = (((1,), (0,)), ((), ()))
VMEM_LIMIT = 16 * 1024 * 1024
VMEM_PACK = 60 * 1024 * 1024
VMEM_ALONE = 32 * 1024 * 1024
VMEM = pl.BlockSpec(memory_space=pltpu.VMEM)
SMEM = pl.BlockSpec(memory_space=pltpu.SMEM)
ANY = pl.BlockSpec(memory_space=pl.ANY)


def dot(a, b, dims):
    return lax.dot_general(a, b, dims, preferred_element_type=jnp.float32)


def kernel_call(kernel, out_shape, operands, flops, transcendentals=0):
    moved = sum(x.size * x.dtype.itemsize for x in operands)
    return pl.pallas_call(
        kernel,
        in_specs=[SMEM if x.dtype == jnp.int32 else VMEM for x in operands],
        out_specs=jax.tree.map(lambda _: VMEM, out_shape),
        out_shape=out_shape,
        compiler_params=pltpu.CompilerParams(vmem_limit_bytes=VMEM_LIMIT),
        cost_estimate=pl.CostEstimate(
            flops=flops, bytes_accessed=moved, transcendentals=transcendentals
        ),
    )(*operands)


def send(array, rule):
    n_ctx, n_head = lax.axis_size("ctx"), lax.axis_size("head")
    pairs = []
    for c in range(n_ctx):
        for h in range(n_head):
            to = rule(c, h)
            if 0 <= to[0] < n_ctx:
                pairs.append((c * n_head + h, to[0] * n_head + to[1]))
    return lax.ppermute(array, BOTH, pairs)


def in_pair(c, h):
    return (c ^ 1, h)


def even_chain(c, h):
    return (c ^ 2, h)


def odd_chain(c, h):
    return (c + 2, h) if c & 2 else (c - 2, h)


def across(c, h):
    return (c + 1, h) if c & 1 else (c - 1, h)


def forward(c, h):
    if h & 1:
        return (c ^ 1, h)
    return (c - 2, h) if c & 1 else (c + 2, h)


def offsets(pos):
    pair = 1 - 2 * lax.rem(pos, 2)
    chain = 2 - 4 * lax.rem(pos // 2, 2)
    return pair, chain, -chain, -pair


def after(value, *others):
    return lax.optimization_barrier((value,) + others)[0]


def pack_kernel(*refs):
    arrays, out_ref, sems = refs[:-2], refs[-2], refs[-1]
    rows = arrays[0].shape[0]
    copies = [
        pltpu.make_async_copy(ref, out_ref.at[n * rows:(n + 1) * rows], sems.at[n])
        for n, ref in enumerate(arrays)
    ]
    for copy in copies:
        copy.start()
    for copy in copies:
        copy.wait()


def pack(*arrays):
    rows, feat = arrays[0].shape
    count = len(arrays)
    return pl.pallas_call(
        pack_kernel,
        in_specs=[ANY] * count,
        out_specs=VMEM,
        out_shape=jax.ShapeDtypeStruct((count * rows, feat), arrays[0].dtype),
        scratch_shapes=[pltpu.SemaphoreType.DMA((count,))],
        compiler_params=pltpu.CompilerParams(vmem_limit_bytes=VMEM_PACK),
        cost_estimate=pl.CostEstimate(
            flops=0, bytes_accessed=4 * count * rows * feat, transcendentals=0
        ),
    )(*arrays)


def begin_kernel(order_ref, w_ref, g_a, g_b, out_ref, kept_ref, used, sems):
    cols = g_a.shape[1]
    copies = []
    for n in range(4):
        start = pl.multiple_of(order_ref[n] * cols, cols)
        to = used.at[n] if n < 2 else kept_ref.at[:, (n - 2) * cols:(n - 1) * cols]
        copies.append(pltpu.make_async_copy(w_ref.at[:, pl.ds(start, cols)], to, sems.at[n]))
        copies[-1].start()
    copies[0].wait()
    total = dot(used[0], g_a[...], NT)
    copies[1].wait()
    out_ref[...] = total + dot(used[1], g_b[...], NT)
    copies[2].wait()
    copies[3].wait()


def begin_project(order, out_weight, g_a, g_b):
    rows, cols = g_a.shape
    feat = out_weight.shape[0]
    return pl.pallas_call(
        begin_kernel,
        in_specs=[SMEM, ANY, VMEM, VMEM],
        out_specs=[VMEM, VMEM],
        out_shape=[
            jax.ShapeDtypeStruct((feat, rows), jnp.float32),
            jax.ShapeDtypeStruct((feat, 2 * cols), out_weight.dtype),
        ],
        scratch_shapes=[
            pltpu.VMEM((2, feat, cols), out_weight.dtype),
            pltpu.SemaphoreType.DMA((4,)),
        ],
        compiler_params=pltpu.CompilerParams(vmem_limit_bytes=VMEM_ALONE),
        cost_estimate=pl.CostEstimate(
            flops=4 * rows * cols * feat, bytes_accessed=8 * feat * cols, transcendentals=0
        ),
    )(order, out_weight, g_a, g_b)


def end_kernel(w_ref, g_a, g_b, begun, out_ref):
    cols = g_a.shape[1]
    total = begun[...] + dot(w_ref[:, :cols], g_a[...], NT)
    out_ref[...] = (total + dot(w_ref[:, cols:], g_b[...], NT)).astype(out_ref.dtype)


def end_project(weight, g_a, g_b, begun):
    rows, cols = g_a.shape
    feat = weight.shape[0]
    return kernel_call(
        end_kernel,
        jax.ShapeDtypeStruct((feat, rows), jnp.bfloat16),
        [weight, g_a, g_b, begun],
        4 * rows * cols * feat,
    )


def columns(head):
    return slice(head * HEAD_DIM, (head + 1) * HEAD_DIM)


def stat_rows(heads):
    return -(-heads * STATS // STAT_TILE) * STAT_TILE


def bias_row(live_flags):
    parts = [
        jnp.full((1, TILE), jnp.where(flag, 0.0, -jnp.inf).astype(jnp.float32))
        for flag in live_flags
    ]
    return jnp.concatenate(parts, axis=1)


def window_bias(mask_ref, pos, tiles, which):
    offs = (0,) + offsets(pos)
    return [
        [
            bias_row(
                [
                    mask_ref[pos * tiles + a, (offs[n] + SPAN) * tiles + b] > 0
                    for a in range(tiles)
                ]
            )
            for b in range(tiles)
        ]
        for n in which
    ]


def source_bias(mask_ref, pos, tiles, which):
    total_tiles = mask_ref.shape[0]
    offs = (0,) + offsets(pos)
    rows = []
    for n in which:
        rows.append([])
        for b in range(tiles):
            flags = []
            for a in range(tiles):
                tile = (pos + offs[n]) * tiles + a
                inside = (tile >= 0) & (tile < total_tiles)
                column = (SPAN - offs[n]) * tiles + b
                flags.append(inside & (mask_ref[jnp.clip(tile, 0, total_tiles - 1), column] > 0))
            rows[-1].append(bias_row(flags))
    return rows


def over_keys(reduce, values):
    return reduce(values.reshape(TILE // 8, 8, values.shape[1]), axis=0)


def softmax_part(scores, biases):
    shifted = []
    top = None
    for block, rows in zip(scores, biases):
        shifted.append([])
        for b, row in enumerate(rows):
            value = block[b * TILE:(b + 1) * TILE] * SCALE_LOG2 + row
            shifted[-1].append(value)
            peak = over_keys(jnp.max, value)
            top = peak if top is None else jnp.maximum(top, peak)
    return shifted, jnp.max(top, axis=0, keepdims=True)


def weighted_values(shifted, top, values_of):
    totals = out = None
    for n, parts in enumerate(shifted):
        weights = []
        for value in parts:
            weight = jnp.exp2(value - top)
            weights.append(weight)
            part = over_keys(jnp.sum, weight)
            totals = part if totals is None else totals + part
        part = dot(values_of(n), jnp.concatenate(weights, axis=0).astype(jnp.bfloat16), TN)
        out = part if out is None else out + part
    return jnp.sum(totals, axis=0, keepdims=True), out


def in_order(steps, ahead_of, finish):
    ahead = ahead_of(*steps[0])
    for at, step in enumerate(steps):
        now = ahead
        if at + 1 < len(steps):
            ahead = ahead_of(*steps[at + 1])
        finish(*step, now)


def forward_kernel(which, pos_ref, mask_ref, *rest):
    windows, (out_ref, run_ref) = rest[:len(which)], rest[len(which):]
    pos = pos_ref[0]
    feat, rows = out_ref.shape
    biases = window_bias(mask_ref, pos, rows // TILE, which)

    def scores_of(head):
        cols = columns(head)
        q = windows[0][2 * rows:, cols]
        return [dot(w[:rows, cols], q, NT) for w in windows]

    def finish(head, scores):
        cols = columns(head)

        def values_of(n):
            return windows[n][rows:2 * rows, cols]

        shifted, top = softmax_part(scores, biases)
        totals, out = weighted_values(shifted, top, values_of)
        out_ref[cols, :] = out
        at = head * RUN_ROWS
        run_ref[at:at + 8, :] = jnp.broadcast_to(top, (8, rows))
        run_ref[at + 8:at + 16, :] = jnp.broadcast_to(totals, (8, rows))

    in_order([(head,) for head in range(feat // HEAD_DIM)], scores_of, finish)


def forward_part(pos, tile_mask, own, which, windows):
    rows, feat = own.shape[0] // 3, own.shape[1]
    heads = feat // HEAD_DIM
    return kernel_call(
        functools.partial(forward_kernel, which),
        [
            jax.ShapeDtypeStruct((feat, rows), jnp.float32),
            jax.ShapeDtypeStruct((heads * RUN_ROWS, rows), jnp.float32),
        ],
        [pos, tile_mask, own, *windows],
        4 * len(which) * rows * rows * feat,
        len(which) * rows * rows * heads,
    )


def statistics_kernel(
    which, pos_ref, mask_ref, own_ref, w_ref, out_in, run_in, d_ref, stats_ref, packed_ref
):
    pos = pos_ref[0]
    feat, rows = d_ref.shape
    biases = window_bias(mask_ref, pos, rows // TILE, [which])

    def scores_of(head):
        cols = columns(head)
        return [dot(w_ref[:rows, cols], own_ref[2 * rows:, cols], NT)]

    def finish(head, scores):
        cols = columns(head)

        def values_of(n):
            return w_ref[rows:, cols]

        at = head * RUN_ROWS
        top_before, totals_before = run_in[at:at + 1, :], run_in[at + 8:at + 9, :]
        shifted, top = softmax_part(scores, biases)
        top = jnp.maximum(top, top_before)
        totals, out = weighted_values(shifted, top, values_of)
        shrink = jnp.exp2(top_before - top)
        totals = totals + totals_before * shrink
        out = out + out_in[cols, :] * shrink
        attn_out = (out / totals).astype(jnp.bfloat16).astype(jnp.float32)
        delta = jnp.sum(d_ref[cols, :].astype(jnp.float32) * attn_out, axis=0, keepdims=True)
        place = head * STATS
        for stat in (top + jnp.log2(totals), delta):
            for _ in range(3):
                piece = stat.astype(jnp.bfloat16).astype(jnp.float32)
                all_stats[0] = jnp.where(row == place, piece, all_stats[0])
                stat = stat - piece
                place += 1
        packed_ref[cols, :] = d_ref[cols, :]

    row = lax.broadcasted_iota(jnp.int32, stats_ref.shape, 0)
    all_stats = [jnp.zeros(stats_ref.shape, jnp.float32)]
    in_order([(head,) for head in range(feat // HEAD_DIM)], scores_of, finish)
    stats_ref[...] = all_stats[0].astype(jnp.bfloat16)
    packed_ref[feat:, :] = all_stats[0].astype(jnp.bfloat16)


def statistics(pos, tile_mask, own, which, window, out, run, d_out_t):
    feat, rows = d_out_t.shape
    heads = feat // HEAD_DIM
    return kernel_call(
        functools.partial(statistics_kernel, which),
        [
            jax.ShapeDtypeStruct((stat_rows(heads), rows), jnp.bfloat16),
            jax.ShapeDtypeStruct((feat + stat_rows(heads), rows), jnp.bfloat16),
        ],
        [pos, tile_mask, own, window, out, run, d_out_t],
        4 * rows * rows * feat,
        rows * rows * heads,
    )


def statistics_of(ref, start, head):
    stats = ref[start:, :].astype(jnp.float32)
    rows = [stats[head * STATS + n:head * STATS + n + 1] for n in range(STATS)]
    return rows[0] + rows[1] + rows[2], rows[3] + rows[4] + rows[5]


def block_grads(scores, dprobs, bias_rows, lse, delta):
    probs = jnp.concatenate(
        [
            jnp.exp2(scores[b * TILE:(b + 1) * TILE] * SCALE_LOG2 + (row - lse))
            for b, row in enumerate(bias_rows)
        ],
        axis=0,
    )
    dscores = probs * (dprobs - delta)
    return probs.astype(jnp.bfloat16), dscores.astype(jnp.bfloat16)


def query_kernel(which, pos_ref, mask_ref, *rest):
    count = len(which)
    windows = rest[:count]
    d_ref, s_ref, dq_ref, dk_ref, dv_ref = rest[count:]
    rows, feat = dq_ref.shape
    biases = window_bias(mask_ref, pos_ref[0], rows // TILE, which)
    sums = [None]

    def keys_of(n, cols):
        return windows[n][:rows, cols]

    def values_of(n, cols):
        return windows[n][rows:2 * rows, cols]

    def queries_of(cols):
        return windows[0][2 * rows:, cols]

    def products(head, n):
        cols = columns(head)
        return (
            dot(keys_of(n, cols), queries_of(cols), NT),
            dot(values_of(n, cols), d_ref[cols, :], NN),
        )

    def finish(head, n, now):
        cols = columns(head)
        probs, dscores = block_grads(*now, biases[n], *statistics_of(s_ref, 0, head))
        part = dot(keys_of(n, cols), dscores, TN)
        if n == 0:
            sums[0] = part
            dk_ref[:, cols] = dot(dscores, queries_of(cols), NN)
            dv_ref[:, cols] = dot(probs, d_ref[cols, :], NT)
        else:
            sums[0] = sums[0] + part
        if n == count - 1:
            dq_ref[:, cols] = jnp.transpose(sums[0] * SCALE).astype(dq_ref.dtype)

    steps = [(head, n) for head in range(feat // HEAD_DIM) for n in range(count)]
    in_order(steps, products, finish)


def query_side(pos, tile_mask, own, which, windows, d_out_t, stats):
    feat, rows = d_out_t.shape
    total = jax.ShapeDtypeStruct((rows, feat), jnp.float32)
    return kernel_call(
        functools.partial(query_kernel, which),
        [jax.ShapeDtypeStruct((rows, feat), jnp.bfloat16), total, total],
        [pos, tile_mask, own, *windows, d_out_t, stats],
        34 * rows * rows * feat,
        5 * rows * rows * feat // HEAD_DIM,
    )


def key_kernel(which, final, pos_ref, mask_ref, own_ref, *rest):
    count = len(which)
    sources = [rest[3 * n:3 * n + 3] for n in range(count)]
    dk_in, dv_in, dk_ref, dv_ref = rest[3 * count:]
    rows, feat = dk_in.shape
    biases = source_bias(mask_ref, pos_ref[0], rows // TILE, which)
    sums = [None, None]

    def products(head, n):
        cols = columns(head)
        q_ref, d_ref, _ = sources[n]
        return (
            dot(own_ref[:rows, cols], q_ref[q_ref.shape[0] - rows:, cols], NT),
            dot(own_ref[rows:2 * rows, cols], d_ref[cols, :], NN),
        )

    def finish(head, n, now):
        cols = columns(head)
        q_ref, d_ref, s_ref = sources[n]
        start = feat if s_ref.shape[0] > feat else 0
        probs, dscores = block_grads(*now, biases[n], *statistics_of(s_ref, start, head))
        before = (dk_in[:, cols], dv_in[:, cols]) if n == 0 else sums
        sums[:] = [
            before[0] + dot(dscores, q_ref[q_ref.shape[0] - rows:, cols], NN),
            before[1] + dot(probs, d_ref[cols, :], NT),
        ]
        if n == count - 1:
            dk, dv = sums
            dk_ref[:, cols] = (dk * SCALE if final else dk).astype(dk_ref.dtype)
            dv_ref[:, cols] = dv.astype(dv_ref.dtype)

    steps = [(head, n) for head in range(feat // HEAD_DIM) for n in range(count)]
    in_order(steps, products, finish)


def key_side(pos, tile_mask, own, sources, begun, final):
    rows, feat = begun[0].shape
    operands = [pos, tile_mask, own]
    for _, q, d, s in sources:
        operands += [q, d, s]
    which = [source[0] for source in sources]
    dtype = jnp.bfloat16 if final else jnp.float32
    return kernel_call(
        functools.partial(key_kernel, which, final),
        [jax.ShapeDtypeStruct((rows, feat), dtype)] * 2,
        operands + list(begun),
        8 * len(which) * rows * rows * feat,
        len(which) * rows * rows * feat // HEAD_DIM,
    )


def local(queries, keys, values, out_weight, reward_grad, tile_mask):
    rows = queries.shape[0]
    ctx = lax.axis_index("ctx").astype(jnp.int32)
    head = lax.axis_index("head").astype(jnp.int32)
    pos = ctx.reshape(1)

    def second_step(x, a, b):
        a_is_held = (ctx % 2 == 0) == (ctx // 2 % 2 == 0)
        return jnp.where(head % 2 == 1, jnp.where(a_is_held, a, b), x)

    far = send(reward_grad, lambda c, h: (c, h ^ 2))
    kvq = pack(keys, values, queries)
    kvq_b = send(kvq, odd_chain)
    kvq_a = send(kvq, even_chain)
    kvq_x = send(kvq, in_pair)
    near = send(after(reward_grad, kvq), lambda c, h: (c, h ^ 1))
    order = jnp.stack([head, head ^ 1, head ^ 2, head ^ 3])
    begun, kept = begin_project(order, out_weight, reward_grad, near)
    far = after(far, begun)
    far_near = send(far, lambda c, h: (c, h ^ 1))
    second = second_step(kvq_x, kvq_a, kvq_b)
    kv_g = send(second[:2 * rows], forward)
    d_out_t = end_project(kept, far, far_near, after(begun, second))
    out, run = forward_part(
        pos, tile_mask, after(kvq, d_out_t), [0, 1, 2, 3], [kvq_x, kvq_a, kvq_b]
    )
    stats, packed = statistics(pos, tile_mask, kvq, 4, kv_g, out, run, d_out_t)
    q_g = send(after(second[2 * rows:], out), forward)
    d_g = send(d_out_t, across)
    p_b = send(packed, odd_chain)
    p_a = send(packed, even_chain)
    p_x = send(packed, in_pair)
    s_g = send(stats, across)
    grad_queries, *begun_keys = query_side(
        pos, tile_mask, kvq, [0, 1, 2, 3, 4], [kvq_x, kvq_a, kvq_b, kv_g], d_out_t,
        after(stats, q_g, d_g),
    )
    grad_keys, grad_values = key_side(
        pos,
        tile_mask,
        kvq,
        [
            (4, q_g, d_g, s_g),
            (1, kvq_x, p_x, p_x),
            (2, kvq_a, p_a, p_a),
            (3, kvq_b, p_b, p_b),
        ],
        begun_keys,
        True,
    )
    return (grad_queries, grad_keys, grad_values)


def solution(mesh):
    placed = (
        P("ctx", "head"),
        P("ctx", "head"),
        P("ctx", "head"),
        P("head", None),
        P("ctx", "head"),
        P(),
    )
    return jax.shard_map(
        local,
        mesh=mesh,
        in_specs=placed,
        out_specs=(P("ctx", "head"), P("ctx", "head"), P("ctx", "head")),
        check_vma=False,
    )
```

```python
import functools
import math

import jax
import jax.numpy as jnp
from jax import lax
from jax.experimental import pallas as pl
from jax.experimental.pallas import tpu as pltpu
from jax.sharding import PartitionSpec as P

HEAD_DIM = 128
TILE = 128
SPAN = 2
RUN_ROWS = 16
STATS = 6
STAT_TILE = 16
BLOCKS = 4
SCALE = 1.0 / math.sqrt(HEAD_DIM)
SCALE_LOG2 = SCALE * math.log2(math.e)
BOTH = ("ctx", "head")
NT = (((1,), (1,)), ((), ()))
TN = (((0,), (0,)), ((), ()))
NN = (((1,), (0,)), ((), ()))
VMEM_LIMIT = 32 * 1024 * 1024
VMEM_PACK = 60 * 1024 * 1024
VMEM_ALONE = 32 * 1024 * 1024
VMEM = pl.BlockSpec(memory_space=pltpu.VMEM)
SMEM = pl.BlockSpec(memory_space=pltpu.SMEM)
ANY = pl.BlockSpec(memory_space=pl.ANY)


def dot(a, b, dims):
    return lax.dot_general(a, b, dims, preferred_element_type=jnp.float32)


def kernel_call(kernel, out_shape, operands, flops, transcendentals=0):
    moved = sum(x.size * x.dtype.itemsize for x in operands)
    return pl.pallas_call(
        kernel,
        in_specs=[SMEM if x.dtype == jnp.int32 else VMEM for x in operands],
        out_specs=jax.tree.map(lambda _: VMEM, out_shape),
        out_shape=out_shape,
        compiler_params=pltpu.CompilerParams(vmem_limit_bytes=VMEM_LIMIT),
        cost_estimate=pl.CostEstimate(
            flops=flops, bytes_accessed=moved, transcendentals=transcendentals
        ),
    )(*operands)


def send(array, rule):
    n_ctx, n_head = lax.axis_size("ctx"), lax.axis_size("head")
    pairs = []
    for c in range(n_ctx):
        for h in range(n_head):
            to = rule(c, h)
            if 0 <= to[0] < n_ctx:
                pairs.append((c * n_head + h, to[0] * n_head + to[1]))
    return lax.ppermute(array, BOTH, pairs)


def in_pair(c, h):
    return (c ^ 1, h)


def even_chain(c, h):
    return (c ^ 2, h)


def odd_chain(c, h):
    return (c + 2, h) if c & 2 else (c - 2, h)


def across(c, h):
    return (c + 1, h) if c & 1 else (c - 1, h)


def forward(c, h):
    if h & 1:
        return (c ^ 1, h)
    return (c - 2, h) if c & 1 else (c + 2, h)


def offsets(pos):
    pair = 1 - 2 * lax.rem(pos, 2)
    chain = 2 - 4 * lax.rem(pos // 2, 2)
    return pair, chain, -chain, -pair


def after(value, *others):
    return lax.optimization_barrier((value,) + others)[0]


def pack_kernel(*refs):
    arrays, out_ref, sems = refs[:-2], refs[-2], refs[-1]
    rows = arrays[0].shape[0]
    copies = [
        pltpu.make_async_copy(ref, out_ref.at[n * rows:(n + 1) * rows], sems.at[n])
        for n, ref in enumerate(arrays)
    ]
    for copy in copies:
        copy.start()
    for copy in copies:
        copy.wait()


def pack(*arrays):
    rows, feat = arrays[0].shape
    count = len(arrays)
    return pl.pallas_call(
        pack_kernel,
        in_specs=[ANY] * count,
        out_specs=VMEM,
        out_shape=jax.ShapeDtypeStruct((count * rows, feat), arrays[0].dtype),
        scratch_shapes=[pltpu.SemaphoreType.DMA((count,))],
        compiler_params=pltpu.CompilerParams(vmem_limit_bytes=VMEM_PACK),
        cost_estimate=pl.CostEstimate(
            flops=0, bytes_accessed=4 * count * rows * feat, transcendentals=0
        ),
    )(*arrays)


def begin_kernel(order_ref, w_ref, g_a, g_b, out_ref, kept_ref, used, sems):
    cols = g_a.shape[1]
    copies = []
    for n in range(4):
        start = pl.multiple_of(order_ref[n] * cols, cols)
        to = used.at[n] if n < 2 else kept_ref.at[:, (n - 2) * cols:(n - 1) * cols]
        copies.append(pltpu.make_async_copy(w_ref.at[:, pl.ds(start, cols)], to, sems.at[n]))
        copies[-1].start()
    copies[0].wait()
    total = dot(used[0], g_a[...], NT)
    copies[1].wait()
    out_ref[...] = total + dot(used[1], g_b[...], NT)
    copies[2].wait()
    copies[3].wait()


def begin_project(order, out_weight, g_a, g_b):
    rows, cols = g_a.shape
    feat = out_weight.shape[0]
    return pl.pallas_call(
        begin_kernel,
        in_specs=[SMEM, ANY, VMEM, VMEM],
        out_specs=[VMEM, VMEM],
        out_shape=[
            jax.ShapeDtypeStruct((feat, rows), jnp.float32),
            jax.ShapeDtypeStruct((feat, 2 * cols), out_weight.dtype),
        ],
        scratch_shapes=[
            pltpu.VMEM((2, feat, cols), out_weight.dtype),
            pltpu.SemaphoreType.DMA((4,)),
        ],
        compiler_params=pltpu.CompilerParams(vmem_limit_bytes=VMEM_ALONE),
        cost_estimate=pl.CostEstimate(
            flops=4 * rows * cols * feat, bytes_accessed=8 * feat * cols, transcendentals=0
        ),
    )(order, out_weight, g_a, g_b)


def end_kernel(w_ref, g_a, g_b, begun, out_ref):
    cols = g_a.shape[1]
    total = begun[...] + dot(w_ref[:, :cols], g_a[...], NT)
    out_ref[...] = (total + dot(w_ref[:, cols:], g_b[...], NT)).astype(out_ref.dtype)


def end_project(weight, g_a, g_b, begun):
    rows, cols = g_a.shape
    feat = weight.shape[0]
    return kernel_call(
        end_kernel,
        jax.ShapeDtypeStruct((feat, rows), jnp.bfloat16),
        [weight, g_a, g_b, begun],
        4 * rows * cols * feat,
    )


def columns(head):
    return slice(head * HEAD_DIM, (head + 1) * HEAD_DIM)


def stat_rows(heads):
    return -(-heads * STATS // STAT_TILE) * STAT_TILE


def block_rows(n, head, rows):
    at = (head * BLOCKS + n) * rows
    return slice(at, at + rows)


def bias_row(live_flags):
    parts = [
        jnp.full((1, TILE), jnp.where(flag, 0.0, -jnp.inf).astype(jnp.float32))
        for flag in live_flags
    ]
    return jnp.concatenate(parts, axis=1)


def window_bias(mask_ref, pos, tiles, which):
    offs = (0,) + offsets(pos)
    return [
        [
            bias_row(
                [
                    mask_ref[pos * tiles + a, (offs[n] + SPAN) * tiles + b] > 0
                    for a in range(tiles)
                ]
            )
            for b in range(tiles)
        ]
        for n in which
    ]


def source_bias(mask_ref, pos, tiles, which):
    total_tiles = mask_ref.shape[0]
    offs = (0,) + offsets(pos)
    rows = []
    for n in which:
        rows.append([])
        for b in range(tiles):
            flags = []
            for a in range(tiles):
                tile = (pos + offs[n]) * tiles + a
                inside = (tile >= 0) & (tile < total_tiles)
                column = (SPAN - offs[n]) * tiles + b
                flags.append(inside & (mask_ref[jnp.clip(tile, 0, total_tiles - 1), column] > 0))
            rows[-1].append(bias_row(flags))
    return rows


def over_keys(reduce, values):
    return reduce(values.reshape(TILE // 8, 8, values.shape[1]), axis=0)


def softmax_part(scores, biases):
    shifted = []
    top = None
    for block, rows in zip(scores, biases):
        shifted.append([])
        for b, row in enumerate(rows):
            value = block[b * TILE:(b + 1) * TILE] * SCALE_LOG2 + row
            shifted[-1].append(value)
            peak = over_keys(jnp.max, value)
            top = peak if top is None else jnp.maximum(top, peak)
    return shifted, jnp.max(top, axis=0, keepdims=True)


def weighted_values(shifted, top, values_of, keep=None):
    totals = out = None
    for n, parts in enumerate(shifted):
        weights = []
        for value in parts:
            weight = jnp.exp2(value - top)
            weights.append(weight)
            part = over_keys(jnp.sum, weight)
            totals = part if totals is None else totals + part
        weights = jnp.concatenate(weights, axis=0)
        if keep is not None:
            keep(n, weights)
        part = dot(values_of(n), weights.astype(jnp.bfloat16), TN)
        out = part if out is None else out + part
    return jnp.sum(totals, axis=0, keepdims=True), out


def in_order(steps, ahead_of, finish):
    ahead = ahead_of(*steps[0])
    for at, step in enumerate(steps):
        now = ahead
        if at + 1 < len(steps):
            ahead = ahead_of(*steps[at + 1])
        finish(*step, now)


def forward_kernel(which, pos_ref, mask_ref, *rest):
    windows, (out_ref, run_ref, kept_ref) = rest[:len(which)], rest[len(which):]
    pos = pos_ref[0]
    feat, rows = out_ref.shape
    biases = window_bias(mask_ref, pos, rows // TILE, which)

    def scores_of(head):
        cols = columns(head)
        q = windows[0][2 * rows:, cols]
        return [dot(w[:rows, cols], q, NT) for w in windows]

    def finish(head, scores):
        cols = columns(head)

        def values_of(n):
            return windows[n][rows:2 * rows, cols]

        def keep(n, weights):
            kept_ref[block_rows(n, head, rows), :] = weights

        shifted, top = softmax_part(scores, biases)
        totals, out = weighted_values(shifted, top, values_of, keep)
        out_ref[cols, :] = out
        at = head * RUN_ROWS
        run_ref[at:at + 8, :] = jnp.broadcast_to(top, (8, rows))
        run_ref[at + 8:at + 16, :] = jnp.broadcast_to(totals, (8, rows))

    in_order([(head,) for head in range(feat // HEAD_DIM)], scores_of, finish)


def forward_part(pos, tile_mask, own, which, windows):
    rows, feat = own.shape[0] // 3, own.shape[1]
    heads = feat // HEAD_DIM
    return kernel_call(
        functools.partial(forward_kernel, which),
        [
            jax.ShapeDtypeStruct((feat, rows), jnp.float32),
            jax.ShapeDtypeStruct((heads * RUN_ROWS, rows), jnp.float32),
            jax.ShapeDtypeStruct((len(which) * feat // HEAD_DIM * rows, rows), jnp.float32),
        ],
        [pos, tile_mask, own, *windows],
        4 * len(which) * rows * rows * feat,
        len(which) * rows * rows * heads,
    )


def statistics_kernel(
    which, pos_ref, mask_ref, own_ref, w_ref, out_in, run_in, d_ref, stats_ref, packed_ref
):
    pos = pos_ref[0]
    feat, rows = d_ref.shape
    biases = window_bias(mask_ref, pos, rows // TILE, [which])

    def scores_of(head):
        cols = columns(head)
        return [dot(w_ref[:rows, cols], own_ref[2 * rows:, cols], NT)]

    def finish(head, scores):
        cols = columns(head)

        def values_of(n):
            return w_ref[rows:, cols]

        at = head * RUN_ROWS
        top_before, totals_before = run_in[at:at + 1, :], run_in[at + 8:at + 9, :]
        shifted, top = softmax_part(scores, biases)
        top = jnp.maximum(top, top_before)
        totals, out = weighted_values(shifted, top, values_of)
        shrink = jnp.exp2(top_before - top)
        totals = totals + totals_before * shrink
        out = out + out_in[cols, :] * shrink
        attn_out = (out / totals).astype(jnp.bfloat16).astype(jnp.float32)
        delta = jnp.sum(d_ref[cols, :].astype(jnp.float32) * attn_out, axis=0, keepdims=True)
        place = head * STATS
        for stat in (top + jnp.log2(totals), delta):
            for _ in range(3):
                piece = stat.astype(jnp.bfloat16).astype(jnp.float32)
                all_stats[0] = jnp.where(row == place, piece, all_stats[0])
                stat = stat - piece
                place += 1
        packed_ref[cols, :] = d_ref[cols, :]

    row = lax.broadcasted_iota(jnp.int32, stats_ref.shape, 0)
    all_stats = [jnp.zeros(stats_ref.shape, jnp.float32)]
    in_order([(head,) for head in range(feat // HEAD_DIM)], scores_of, finish)
    stats_ref[...] = all_stats[0].astype(jnp.bfloat16)
    packed_ref[feat:, :] = all_stats[0].astype(jnp.bfloat16)


def statistics(pos, tile_mask, own, which, window, out, run, d_out_t):
    feat, rows = d_out_t.shape
    heads = feat // HEAD_DIM
    return kernel_call(
        functools.partial(statistics_kernel, which),
        [
            jax.ShapeDtypeStruct((stat_rows(heads), rows), jnp.bfloat16),
            jax.ShapeDtypeStruct((feat + stat_rows(heads), rows), jnp.bfloat16),
        ],
        [pos, tile_mask, own, window, out, run, d_out_t],
        4 * rows * rows * feat,
        rows * rows * heads,
    )


def statistics_of(ref, start, head):
    stats = ref[start:, :].astype(jnp.float32)
    rows = [stats[head * STATS + n:head * STATS + n + 1] for n in range(STATS)]
    return rows[0] + rows[1] + rows[2], rows[3] + rows[4] + rows[5]


def block_grads(scores, dprobs, bias_rows, lse, delta):
    probs = jnp.concatenate(
        [
            jnp.exp2(scores[b * TILE:(b + 1) * TILE] * SCALE_LOG2 + (row - lse))
            for b, row in enumerate(bias_rows)
        ],
        axis=0,
    )
    dscores = probs * (dprobs - delta)
    return probs.astype(jnp.bfloat16), dscores.astype(jnp.bfloat16)


def query_kernel(which, pos_ref, mask_ref, own_ref, *rest):
    windows, rest = (own_ref,) + rest[:BLOCKS], rest[BLOCKS:]
    d_ref, s_ref, run_ref, kept_ref, q_last, d_last, *outs = rest
    dq_ref, dk_ref, dv_ref, scores_ref, dprobs_ref = outs
    rows, feat = dq_ref.shape
    last_bias = window_bias(mask_ref, pos_ref[0], rows // TILE, which[BLOCKS:])[0]
    sums = [None]

    def products(head, n):
        cols = columns(head)
        keys, values = own_ref[:rows, cols], own_ref[rows:2 * rows, cols]
        queries = own_ref[2 * rows:, cols]
        if n < BLOCKS:
            others = q_last[:, cols] if n == BLOCKS - 1 else windows[n + 1][2 * rows:, cols]
            scores_ref[block_rows(n, head, rows), :] = dot(keys, others, NT)
            scores = None
        else:
            dprobs_ref[head * rows:(head + 1) * rows, :] = dot(values, d_last[cols, :], NN)
            scores = dot(windows[n][:rows, cols], queries, NT)
        return scores, dot(windows[n][rows:2 * rows, cols], d_ref[cols, :], NN)

    def finish(head, n, now):
        cols = columns(head)
        scores, dprobs = now
        lse, delta = statistics_of(s_ref, 0, head)
        if n < BLOCKS:
            at = head * RUN_ROWS
            factor = jnp.exp2(run_ref[at:at + 1, :] - lse)
            probs = kept_ref[block_rows(n, head, rows), :] * factor
            dscores = (probs * (dprobs - delta)).astype(jnp.bfloat16)
        else:
            _, dscores = block_grads(scores, dprobs, last_bias, lse, delta)
        part = dot(windows[n][:rows, cols], dscores, TN)
        if n == 0:
            sums[0] = part
            dk_ref[:, cols] = dot(dscores, own_ref[2 * rows:, cols], NN)
            dv_ref[:, cols] = dot(probs.astype(jnp.bfloat16), d_ref[cols, :], NT)
        else:
            sums[0] = sums[0] + part
        if n == BLOCKS:
            dq_ref[:, cols] = jnp.transpose(sums[0] * SCALE).astype(dq_ref.dtype)

    steps = [(head, n) for head in range(feat // HEAD_DIM) for n in range(BLOCKS + 1)]
    in_order(steps, products, finish)


def query_side(pos, tile_mask, own, which, windows, d_out_t, stats, run, kept, q_last, d_last):
    feat, rows = d_out_t.shape
    heads = feat // HEAD_DIM
    total = jax.ShapeDtypeStruct((rows, feat), jnp.float32)
    return kernel_call(
        functools.partial(query_kernel, which),
        [
            jax.ShapeDtypeStruct((rows, feat), jnp.bfloat16),
            total,
            total,
            jax.ShapeDtypeStruct((heads * BLOCKS * rows, rows), jnp.float32),
            jax.ShapeDtypeStruct((heads * rows, rows), jnp.float32),
        ],
        [pos, tile_mask, own, *windows, d_out_t, stats, run, kept, q_last, d_last],
        36 * rows * rows * feat,
        rows * rows * heads,
    )


def key_kernel(which, pos_ref, mask_ref, own_ref, *rest):
    sources = [rest[3 * n:3 * n + 3] for n in range(BLOCKS)]
    scores_ref, dprobs_ref, dk_in, dv_in, dk_out, dv_out, dk_ref, dv_ref, sems = rest[3 * BLOCKS:]
    copies = []
    rows, feat = dk_in.shape
    biases = source_bias(mask_ref, pos_ref[0], rows // TILE, which)
    sums = [None, None]

    def products(head, n):
        cols = columns(head)
        if n == BLOCKS - 1:
            return dprobs_ref[head * rows:(head + 1) * rows, :]
        return dot(own_ref[rows:2 * rows, cols], sources[n][1][cols, :], NN)

    def finish(head, n, dprobs):
        cols = columns(head)
        q_ref, d_ref, s_ref = sources[n]
        start = feat if s_ref.shape[0] > feat else 0
        scores = scores_ref[block_rows(n, head, rows), :]
        probs, dscores = block_grads(
            scores, dprobs, biases[n], *statistics_of(s_ref, start, head)
        )
        before = (dk_in[:, cols], dv_in[:, cols]) if n == 0 else sums
        sums[:] = [
            before[0] + dot(dscores, q_ref[q_ref.shape[0] - rows:, cols], NN),
            before[1] + dot(probs, d_ref[cols, :], NT),
        ]
        if n == BLOCKS - 1:
            dk, dv = sums
            dk_ref[:, cols] = (dk * SCALE).astype(dk_ref.dtype)
            dv_ref[:, cols] = dv.astype(dv_ref.dtype)
            for which_out, (from_ref, to_ref) in enumerate(((dk_ref, dk_out), (dv_ref, dv_out))):
                copies.append(
                    pltpu.make_async_copy(
                        from_ref.at[:, cols], to_ref.at[:, cols], sems.at[2 * head + which_out]
                    )
                )
                copies[-1].start()

    steps = [(head, n) for head in range(feat // HEAD_DIM) for n in range(BLOCKS)]
    in_order(steps, products, finish)
    for copy in copies:
        copy.wait()


def key_side(pos, tile_mask, own, sources, scores, dprobs, begun):
    rows, feat = begun[0].shape
    operands = [pos, tile_mask, own]
    for _, q, d, s in sources:
        operands += [q, d, s]
    operands += [scores, dprobs, *begun]
    return pl.pallas_call(
        functools.partial(key_kernel, [source[0] for source in sources]),
        in_specs=[SMEM if x.dtype == jnp.int32 else VMEM for x in operands],
        out_specs=[ANY] * 2,
        out_shape=[jax.ShapeDtypeStruct((rows, feat), jnp.bfloat16)] * 2,
        scratch_shapes=[
            pltpu.VMEM((rows, feat), jnp.bfloat16),
            pltpu.VMEM((rows, feat), jnp.bfloat16),
            pltpu.SemaphoreType.DMA((2 * feat // HEAD_DIM,)),
        ],
        compiler_params=pltpu.CompilerParams(vmem_limit_bytes=VMEM_LIMIT),
        cost_estimate=pl.CostEstimate(
            flops=26 * rows * rows * feat,
            bytes_accessed=sum(x.size * x.dtype.itemsize for x in operands),
            transcendentals=BLOCKS * rows * rows * feat // HEAD_DIM,
        ),
    )(*operands)


def local(queries, keys, values, out_weight, reward_grad, tile_mask):
    rows = queries.shape[0]
    ctx = lax.axis_index("ctx").astype(jnp.int32)
    head = lax.axis_index("head").astype(jnp.int32)
    pos = ctx.reshape(1)

    def second_step(x, a, b):
        a_is_held = (ctx % 2 == 0) == (ctx // 2 % 2 == 0)
        return jnp.where(head % 2 == 1, jnp.where(a_is_held, a, b), x)

    far = send(reward_grad, lambda c, h: (c, h ^ 2))
    kvq = pack(keys, values, queries)
    kvq_b = send(kvq, odd_chain)
    kvq_a = send(kvq, even_chain)
    kvq_x = send(kvq, in_pair)
    near = send(after(reward_grad, kvq), lambda c, h: (c, h ^ 1))
    order = jnp.stack([head, head ^ 1, head ^ 2, head ^ 3])
    begun, kept = begin_project(order, out_weight, reward_grad, near)
    far = after(far, begun)
    far_near = send(far, lambda c, h: (c, h ^ 1))
    second = second_step(kvq_x, kvq_a, kvq_b)
    kv_g = send(second[:2 * rows], forward)
    d_out_t = end_project(kept, far, far_near, after(begun, second))
    out, run, kept_weights = forward_part(
        pos, tile_mask, after(kvq, d_out_t), [0, 2, 1, 3], [kvq_a, kvq_x, kvq_b]
    )
    stats, packed = statistics(pos, tile_mask, kvq, 4, kv_g, out, run, d_out_t)
    q_g = send(after(second[2 * rows:], out), forward)
    d_g = send(d_out_t, across)
    p_b = send(packed, odd_chain)
    p_a = send(packed, even_chain)
    p_x = send(packed, in_pair)
    s_g = send(stats, across)
    grad_queries, *begun_keys, scores, dprobs = query_side(
        pos, tile_mask, kvq, [0, 2, 1, 3, 4], [kvq_a, kvq_x, kvq_b, kv_g], d_out_t,
        stats, run, kept_weights, q_g, d_g,
    )
    grad_keys, grad_values = key_side(
        pos,
        tile_mask,
        kvq,
        [
            (2, kvq_a, p_a, p_a),
            (1, kvq_x, p_x, p_x),
            (3, kvq_b, p_b, p_b),
            (4, q_g, d_g, s_g),
        ],
        scores,
        dprobs,
        begun_keys,
    )
    return (grad_queries, grad_keys, grad_values)


def solution(mesh):
    placed = (
        P("ctx", "head"),
        P("ctx", "head"),
        P("ctx", "head"),
        P("head", None),
        P("ctx", "head"),
        P(),
    )
    return jax.shard_map(
        local,
        mesh=mesh,
        in_specs=placed,
        out_specs=(P("ctx", "head"), P("ctx", "head"), P("ctx", "head")),
        check_vma=False,
    )
```

```python
import functools
import math

import jax
import jax.numpy as jnp
from jax import lax
from jax.experimental import pallas as pl
from jax.experimental.pallas import tpu as pltpu
from jax.sharding import PartitionSpec as P

HEAD_DIM = 128
TILE = 128
SPAN = 2
RUN_ROWS = 16
STATS = 6
STAT_TILE = 16
BLOCKS = 4
SCALE = 1.0 / math.sqrt(HEAD_DIM)
SCALE_LOG2 = SCALE * math.log2(math.e)
BOTH = ("ctx", "head")
NT = (((1,), (1,)), ((), ()))
TN = (((0,), (0,)), ((), ()))
NN = (((1,), (0,)), ((), ()))
VMEM_LIMIT = 32 * 1024 * 1024
VMEM_PACK = 60 * 1024 * 1024
VMEM_ALONE = 32 * 1024 * 1024
VMEM = pl.BlockSpec(memory_space=pltpu.VMEM)
SMEM = pl.BlockSpec(memory_space=pltpu.SMEM)
ANY = pl.BlockSpec(memory_space=pl.ANY)


def dot(a, b, dims):
    return lax.dot_general(a, b, dims, preferred_element_type=jnp.float32)


def kernel_call(kernel, out_shape, operands, flops, transcendentals=0):
    moved = sum(x.size * x.dtype.itemsize for x in operands)
    return pl.pallas_call(
        kernel,
        in_specs=[SMEM if x.dtype == jnp.int32 else VMEM for x in operands],
        out_specs=jax.tree.map(lambda _: VMEM, out_shape),
        out_shape=out_shape,
        compiler_params=pltpu.CompilerParams(vmem_limit_bytes=VMEM_LIMIT),
        cost_estimate=pl.CostEstimate(
            flops=flops, bytes_accessed=moved, transcendentals=transcendentals
        ),
    )(*operands)


def send(array, rule):
    n_ctx, n_head = lax.axis_size("ctx"), lax.axis_size("head")
    pairs = []
    for c in range(n_ctx):
        for h in range(n_head):
            to = rule(c, h)
            if 0 <= to[0] < n_ctx:
                pairs.append((c * n_head + h, to[0] * n_head + to[1]))
    return lax.ppermute(array, BOTH, pairs)


def in_pair(c, h):
    return (c ^ 1, h)


def even_chain(c, h):
    return (c ^ 2, h)


def odd_chain(c, h):
    return (c + 2, h) if c & 2 else (c - 2, h)


def across(c, h):
    return (c + 1, h) if c & 1 else (c - 1, h)


def forward(c, h):
    if h & 1:
        return (c ^ 1, h)
    return (c - 2, h) if c & 1 else (c + 2, h)


def offsets(pos):
    pair = 1 - 2 * lax.rem(pos, 2)
    chain = 2 - 4 * lax.rem(pos // 2, 2)
    return pair, chain, -chain, -pair


def after(value, *others):
    return lax.optimization_barrier((value,) + others)[0]


def pack_kernel(*refs):
    arrays, out_ref, sems = refs[:-2], refs[-2], refs[-1]
    rows = arrays[0].shape[0]
    copies = [
        pltpu.make_async_copy(ref, out_ref.at[n * rows:(n + 1) * rows], sems.at[n])
        for n, ref in enumerate(arrays)
    ]
    for copy in copies:
        copy.start()
    for copy in copies:
        copy.wait()


def pack(*arrays):
    rows, feat = arrays[0].shape
    count = len(arrays)
    return pl.pallas_call(
        pack_kernel,
        in_specs=[ANY] * count,
        out_specs=VMEM,
        out_shape=jax.ShapeDtypeStruct((count * rows, feat), arrays[0].dtype),
        scratch_shapes=[pltpu.SemaphoreType.DMA((count,))],
        compiler_params=pltpu.CompilerParams(vmem_limit_bytes=VMEM_PACK),
        cost_estimate=pl.CostEstimate(
            flops=0, bytes_accessed=4 * count * rows * feat, transcendentals=0
        ),
    )(*arrays)


def begin_kernel(order_ref, w_ref, g_a, g_b, out_ref, kept_ref, used, sems):
    cols = g_a.shape[1]
    copies = []
    for n in range(4):
        start = pl.multiple_of(order_ref[n] * cols, cols)
        to = used.at[n] if n < 2 else kept_ref.at[:, (n - 2) * cols:(n - 1) * cols]
        copies.append(pltpu.make_async_copy(w_ref.at[:, pl.ds(start, cols)], to, sems.at[n]))
        copies[-1].start()
    copies[0].wait()
    total = dot(used[0], g_a[...], NT)
    copies[1].wait()
    out_ref[...] = total + dot(used[1], g_b[...], NT)
    copies[2].wait()
    copies[3].wait()


def begin_project(order, out_weight, g_a, g_b):
    rows, cols = g_a.shape
    feat = out_weight.shape[0]
    return pl.pallas_call(
        begin_kernel,
        in_specs=[SMEM, ANY, VMEM, VMEM],
        out_specs=[VMEM, VMEM],
        out_shape=[
            jax.ShapeDtypeStruct((feat, rows), jnp.float32),
            jax.ShapeDtypeStruct((feat, 2 * cols), out_weight.dtype),
        ],
        scratch_shapes=[
            pltpu.VMEM((2, feat, cols), out_weight.dtype),
            pltpu.SemaphoreType.DMA((4,)),
        ],
        compiler_params=pltpu.CompilerParams(vmem_limit_bytes=VMEM_ALONE),
        cost_estimate=pl.CostEstimate(
            flops=4 * rows * cols * feat, bytes_accessed=8 * feat * cols, transcendentals=0
        ),
    )(order, out_weight, g_a, g_b)


def end_kernel(w_ref, g_a, g_b, begun, out_ref):
    cols = g_a.shape[1]
    total = begun[...] + dot(w_ref[:, :cols], g_a[...], NT)
    out_ref[...] = (total + dot(w_ref[:, cols:], g_b[...], NT)).astype(out_ref.dtype)


def end_project(weight, g_a, g_b, begun):
    rows, cols = g_a.shape
    feat = weight.shape[0]
    return kernel_call(
        end_kernel,
        jax.ShapeDtypeStruct((feat, rows), jnp.bfloat16),
        [weight, g_a, g_b, begun],
        4 * rows * cols * feat,
    )


def columns(head):
    return slice(head * HEAD_DIM, (head + 1) * HEAD_DIM)


def stat_rows(heads):
    return -(-heads * STATS // STAT_TILE) * STAT_TILE


def block_rows(n, head, rows):
    at = (head * BLOCKS + n) * rows
    return slice(at, at + rows)


def bias_row(live_flags):
    parts = [
        jnp.full((1, TILE), jnp.where(flag, 0.0, -jnp.inf).astype(jnp.float32))
        for flag in live_flags
    ]
    return jnp.concatenate(parts, axis=1)


def bias_kernel(pos_ref, mask_ref, window_ref, source_ref):
    pos = pos_ref[0]
    rows = window_ref.shape[1]
    tiles = rows // TILE
    total_tiles = mask_ref.shape[0]
    window_ref[...] = jnp.zeros_like(window_ref)
    source_ref[...] = jnp.zeros_like(source_ref)
    for n, off in enumerate((0,) + offsets(pos)):
        for b in range(tiles):
            at = slice(n * tiles + b, n * tiles + b + 1)
            column = (off + SPAN) * tiles + b
            window_ref[at, :] = bias_row(
                [mask_ref[pos * tiles + a, column] > 0 for a in range(tiles)]
            )
            flags = []
            for a in range(tiles):
                tile = (pos + off) * tiles + a
                inside = (tile >= 0) & (tile < total_tiles)
                column = (SPAN - off) * tiles + b
                flags.append(inside & (mask_ref[jnp.clip(tile, 0, total_tiles - 1), column] > 0))
            source_ref[at, :] = bias_row(flags)


def biases_of(pos, tile_mask, rows):
    count = -(-(2 * SPAN + 1) * (rows // TILE) // 8) * 8
    shape = jax.ShapeDtypeStruct((count, rows), jnp.float32)
    return kernel_call(bias_kernel, [shape, shape], [pos, tile_mask], 0)


def bias_rows(ref, which):
    tiles = ref.shape[1] // TILE
    return [[ref[n * tiles + b:n * tiles + b + 1, :] for b in range(tiles)] for n in which]


def over_keys(reduce, values):
    return reduce(values.reshape(TILE // 8, 8, values.shape[1]), axis=0)


def softmax_part(scores, biases):
    shifted = []
    top = None
    for block, rows in zip(scores, biases):
        shifted.append([])
        for b, row in enumerate(rows):
            value = block[b * TILE:(b + 1) * TILE] * SCALE_LOG2 + row
            shifted[-1].append(value)
            peak = over_keys(jnp.max, value)
            top = peak if top is None else jnp.maximum(top, peak)
    return shifted, jnp.max(top, axis=0, keepdims=True)


def weighted_values(shifted, top, values_of, keep=None):
    totals = None
    blocks = []
    for n, parts in enumerate(shifted):
        weights = []
        for value in parts:
            weight = jnp.exp2(value - top)
            weights.append(weight)
            part = over_keys(jnp.sum, weight)
            totals = part if totals is None else totals + part
        weights = jnp.concatenate(weights, axis=0)
        if keep is not None:
            keep(n, weights)
        blocks.append(weights.astype(jnp.bfloat16))
    values = jnp.concatenate([values_of(n) for n in range(len(blocks))], axis=0)
    out = dot(values, jnp.concatenate(blocks, axis=0), TN)
    return jnp.sum(totals, axis=0, keepdims=True), out


def in_order(steps, ahead_of, finish):
    ahead = ahead_of(*steps[0])
    for at, step in enumerate(steps):
        now = ahead
        if at + 1 < len(steps):
            ahead = ahead_of(*steps[at + 1])
        finish(*step, now)


def forward_kernel(which, bias_ref, *rest):
    windows, (out_ref, run_ref, kept_ref) = rest[:len(which)], rest[len(which):]
    feat, rows = out_ref.shape
    biases = bias_rows(bias_ref, which)

    def scores_of(head):
        cols = columns(head)
        q = windows[0][2 * rows:, cols]
        return [dot(w[:rows, cols], q, NT) for w in windows]

    def finish(head, scores):
        cols = columns(head)

        def values_of(n):
            return windows[n][rows:2 * rows, cols]

        def keep(n, weights):
            kept_ref[block_rows(n, head, rows), :] = weights

        shifted, top = softmax_part(scores, biases)
        totals, out = weighted_values(shifted, top, values_of, keep)
        out_ref[cols, :] = out
        at = head * RUN_ROWS
        run_ref[at:at + 8, :] = jnp.broadcast_to(top, (8, rows))
        run_ref[at + 8:at + 16, :] = jnp.broadcast_to(totals, (8, rows))

    in_order([(head,) for head in range(feat // HEAD_DIM)], scores_of, finish)


def forward_part(bias, own, which, windows):
    rows, feat = own.shape[0] // 3, own.shape[1]
    heads = feat // HEAD_DIM
    return kernel_call(
        functools.partial(forward_kernel, which),
        [
            jax.ShapeDtypeStruct((feat, rows), jnp.float32),
            jax.ShapeDtypeStruct((heads * RUN_ROWS, rows), jnp.float32),
            jax.ShapeDtypeStruct((len(which) * feat // HEAD_DIM * rows, rows), jnp.float32),
        ],
        [bias, own, *windows],
        4 * len(which) * rows * rows * feat,
        len(which) * rows * rows * heads,
    )


def statistics_kernel(
    which, bias_ref, own_ref, w_ref, out_in, run_in, d_ref, stats_ref, packed_ref
):
    feat, rows = d_ref.shape
    biases = bias_rows(bias_ref, [which])

    def scores_of(head):
        cols = columns(head)
        return [dot(w_ref[:rows, cols], own_ref[2 * rows:, cols], NT)]

    def finish(head, scores):
        cols = columns(head)

        def values_of(n):
            return w_ref[rows:, cols]

        at = head * RUN_ROWS
        top_before, totals_before = run_in[at:at + 1, :], run_in[at + 8:at + 9, :]
        shifted, top = softmax_part(scores, biases)
        top = jnp.maximum(top, top_before)
        totals, out = weighted_values(shifted, top, values_of)
        shrink = jnp.exp2(top_before - top)
        totals = totals + totals_before * shrink
        out = out + out_in[cols, :] * shrink
        attn_out = (out / totals).astype(jnp.bfloat16).astype(jnp.float32)
        delta = jnp.sum(d_ref[cols, :].astype(jnp.float32) * attn_out, axis=0, keepdims=True)
        place = head * STATS
        for stat in (top + jnp.log2(totals), delta):
            for _ in range(3):
                piece = stat.astype(jnp.bfloat16).astype(jnp.float32)
                all_stats[0] = jnp.where(row == place, piece, all_stats[0])
                stat = stat - piece
                place += 1
        packed_ref[cols, :] = d_ref[cols, :]

    row = lax.broadcasted_iota(jnp.int32, stats_ref.shape, 0)
    all_stats = [jnp.zeros(stats_ref.shape, jnp.float32)]
    in_order([(head,) for head in range(feat // HEAD_DIM)], scores_of, finish)
    stats_ref[...] = all_stats[0].astype(jnp.bfloat16)
    packed_ref[feat:, :] = all_stats[0].astype(jnp.bfloat16)


def statistics(bias, own, which, window, out, run, d_out_t):
    feat, rows = d_out_t.shape
    heads = feat // HEAD_DIM
    return kernel_call(
        functools.partial(statistics_kernel, which),
        [
            jax.ShapeDtypeStruct((stat_rows(heads), rows), jnp.bfloat16),
            jax.ShapeDtypeStruct((feat + stat_rows(heads), rows), jnp.bfloat16),
        ],
        [bias, own, window, out, run, d_out_t],
        4 * rows * rows * feat,
        rows * rows * heads,
    )


def statistics_of(ref, start, head):
    stats = ref[start:, :].astype(jnp.float32)
    rows = [stats[head * STATS + n:head * STATS + n + 1] for n in range(STATS)]
    return rows[0] + rows[1] + rows[2], rows[3] + rows[4] + rows[5]


def block_grads(scores, dprobs, bias_rows, lse, delta):
    probs = jnp.concatenate(
        [
            jnp.exp2(scores[b * TILE:(b + 1) * TILE] * SCALE_LOG2 + (row - lse))
            for b, row in enumerate(bias_rows)
        ],
        axis=0,
    )
    dscores = probs * (dprobs - delta)
    return probs.astype(jnp.bfloat16), dscores.astype(jnp.bfloat16)


def query_kernel(which, bias_ref, own_ref, *rest):
    windows, rest = (own_ref,) + rest[:BLOCKS], rest[BLOCKS:]
    d_ref, s_ref, run_ref, kept_ref, q_last, d_last, *outs = rest
    dq_ref, dk_ref, dv_ref, scores_ref, dprobs_ref = outs
    rows, feat = dq_ref.shape
    last_bias = bias_rows(bias_ref, which[BLOCKS:])[0]

    def products(head):
        cols = columns(head)
        keys, values = own_ref[:rows, cols], own_ref[rows:2 * rows, cols]
        queries = own_ref[2 * rows:, cols]
        for n in range(BLOCKS):
            others = q_last[:, cols] if n == BLOCKS - 1 else windows[n + 1][2 * rows:, cols]
            scores_ref[block_rows(n, head, rows), :] = dot(keys, others, NT)
        dprobs_ref[head * rows:(head + 1) * rows, :] = dot(values, d_last[cols, :], NN)
        scores = dot(windows[BLOCKS][:rows, cols], queries, NT)
        return scores, [dot(w[rows:2 * rows, cols], d_ref[cols, :], NN) for w in windows]

    def finish(head, now):
        cols = columns(head)
        scores, dprobs = now
        lse, delta = statistics_of(s_ref, 0, head)
        at = head * RUN_ROWS
        factor = jnp.exp2(run_ref[at:at + 1, :] - lse)
        dscores = []
        for n in range(BLOCKS):
            probs = kept_ref[block_rows(n, head, rows), :] * factor
            dscores.append((probs * (dprobs[n] - delta)).astype(jnp.bfloat16))
            if n == 0:
                dv_ref[:, cols] = dot(probs.astype(jnp.bfloat16), d_ref[cols, :], NT)
        dk_ref[:, cols] = dot(dscores[0], own_ref[2 * rows:, cols], NN)
        dscores.append(block_grads(scores, dprobs[BLOCKS], last_bias, lse, delta)[1])
        keys = jnp.concatenate([w[:rows, cols] for w in windows], axis=0)
        dq = dot(keys, jnp.concatenate(dscores, axis=0), TN)
        dq_ref[:, cols] = jnp.transpose(dq * SCALE).astype(dq_ref.dtype)

    in_order([(head,) for head in range(feat // HEAD_DIM)], products, finish)


def query_side(bias, own, which, windows, d_out_t, stats, run, kept, q_last, d_last):
    feat, rows = d_out_t.shape
    heads = feat // HEAD_DIM
    total = jax.ShapeDtypeStruct((rows, feat), jnp.float32)
    return kernel_call(
        functools.partial(query_kernel, which),
        [
            jax.ShapeDtypeStruct((rows, feat), jnp.bfloat16),
            total,
            total,
            jax.ShapeDtypeStruct((heads * BLOCKS * rows, rows), jnp.float32),
            jax.ShapeDtypeStruct((heads * rows, rows), jnp.float32),
        ],
        [bias, own, *windows, d_out_t, stats, run, kept, q_last, d_last],
        36 * rows * rows * feat,
        rows * rows * heads,
    )


def key_kernel(which, bias_ref, own_ref, *rest):
    sources = [rest[3 * n:3 * n + 3] for n in range(BLOCKS)]
    scores_ref, dprobs_ref, dk_in, dv_in, dk_out, dv_out, dk_ref, dv_ref, sems = rest[3 * BLOCKS:]
    copies = []
    rows, feat = dk_in.shape
    biases = bias_rows(bias_ref, which)

    def products(head):
        cols = columns(head)
        values = own_ref[rows:2 * rows, cols]
        dprobs = [dot(values, sources[n][1][cols, :], NN) for n in range(BLOCKS - 1)]
        return dprobs + [dprobs_ref[head * rows:(head + 1) * rows, :]]

    def finish(head, dprobs):
        cols = columns(head)
        blocks = []
        for n, (_, _, s_ref) in enumerate(sources):
            start = feat if s_ref.shape[0] > feat else 0
            scores = scores_ref[block_rows(n, head, rows), :]
            blocks.append(
                block_grads(scores, dprobs[n], biases[n], *statistics_of(s_ref, start, head))
            )
        probs, dscores = (jnp.concatenate(parts, axis=1) for parts in zip(*blocks))
        queries = jnp.concatenate([q[q.shape[0] - rows:, cols] for q, _, _ in sources], axis=0)
        grads = jnp.concatenate([d[cols, :] for _, d, _ in sources], axis=1)
        dk = dk_in[:, cols] + dot(dscores, queries, NN)
        dv = dv_in[:, cols] + dot(probs, grads, NT)
        dk_ref[:, cols] = (dk * SCALE).astype(dk_ref.dtype)
        dv_ref[:, cols] = dv.astype(dv_ref.dtype)
        for which_out, (from_ref, to_ref) in enumerate(((dk_ref, dk_out), (dv_ref, dv_out))):
            copies.append(
                pltpu.make_async_copy(
                    from_ref.at[:, cols], to_ref.at[:, cols], sems.at[2 * head + which_out]
                )
            )
            copies[-1].start()

    in_order([(head,) for head in range(feat // HEAD_DIM)], products, finish)
    for copy in copies:
        copy.wait()


def key_side(bias, own, sources, scores, dprobs, begun):
    rows, feat = begun[0].shape
    operands = [bias, own]
    for _, q, d, s in sources:
        operands += [q, d, s]
    operands += [scores, dprobs, *begun]
    return pl.pallas_call(
        functools.partial(key_kernel, [source[0] for source in sources]),
        in_specs=[VMEM] * len(operands),
        out_specs=[ANY] * 2,
        out_shape=[jax.ShapeDtypeStruct((rows, feat), jnp.bfloat16)] * 2,
        scratch_shapes=[
            pltpu.VMEM((rows, feat), jnp.bfloat16),
            pltpu.VMEM((rows, feat), jnp.bfloat16),
            pltpu.SemaphoreType.DMA((2 * feat // HEAD_DIM,)),
        ],
        compiler_params=pltpu.CompilerParams(vmem_limit_bytes=VMEM_LIMIT),
        cost_estimate=pl.CostEstimate(
            flops=26 * rows * rows * feat,
            bytes_accessed=sum(x.size * x.dtype.itemsize for x in operands),
            transcendentals=BLOCKS * rows * rows * feat // HEAD_DIM,
        ),
    )(*operands)


def local(queries, keys, values, out_weight, reward_grad, tile_mask):
    rows = queries.shape[0]
    ctx = lax.axis_index("ctx").astype(jnp.int32)
    head = lax.axis_index("head").astype(jnp.int32)
    pos = ctx.reshape(1)

    def second_step(x, a, b):
        a_is_held = (ctx % 2 == 0) == (ctx // 2 % 2 == 0)
        return jnp.where(head % 2 == 1, jnp.where(a_is_held, a, b), x)

    far = send(reward_grad, lambda c, h: (c, h ^ 2))
    kvq = pack(keys, values, queries)
    kvq_b = send(kvq, odd_chain)
    kvq_a = send(kvq, even_chain)
    kvq_x = send(kvq, in_pair)
    near = send(after(reward_grad, kvq), lambda c, h: (c, h ^ 1))
    order = jnp.stack([head, head ^ 1, head ^ 2, head ^ 3])
    own_bias, other_bias = biases_of(pos, tile_mask, rows)
    near = after(near, own_bias, other_bias)
    begun, kept = begin_project(order, out_weight, reward_grad, near)
    far = after(far, begun)
    far_near = send(far, lambda c, h: (c, h ^ 1))
    second = second_step(kvq_x, kvq_a, kvq_b)
    kv_g = send(second[:2 * rows], forward)
    d_out_t = end_project(kept, far, far_near, after(begun, second))
    out, run, kept_weights = forward_part(
        own_bias, after(kvq, d_out_t), [0, 2, 1, 3], [kvq_a, kvq_x, kvq_b]
    )
    stats, packed = statistics(own_bias, kvq, 4, kv_g, out, run, d_out_t)
    q_g = send(after(second[2 * rows:], out), forward)
    d_g = send(d_out_t, across)
    p_b = send(packed, odd_chain)
    p_a = send(packed, even_chain)
    p_x = send(packed, in_pair)
    s_g = send(stats, across)
    grad_queries, *begun_keys, scores, dprobs = query_side(
        own_bias, kvq, [0, 2, 1, 3, 4], [kvq_a, kvq_x, kvq_b, kv_g], d_out_t,
        stats, run, kept_weights, q_g, d_g,
    )
    grad_keys, grad_values = key_side(
        other_bias,
        kvq,
        [
            (2, kvq_a, p_a, p_a),
            (1, kvq_x, p_x, p_x),
            (3, kvq_b, p_b, p_b),
            (4, q_g, d_g, s_g),
        ],
        scores,
        dprobs,
        begun_keys,
    )
    return (grad_queries, grad_keys, grad_values)


def solution(mesh):
    placed = (
        P("ctx", "head"),
        P("ctx", "head"),
        P("ctx", "head"),
        P("head", None),
        P("ctx", "head"),
        P(),
    )
    return jax.shard_map(
        local,
        mesh=mesh,
        in_specs=placed,
        out_specs=(P("ctx", "head"), P("ctx", "head"), P("ctx", "head")),
        check_vma=False,
    )
```

```python
import functools
import math

import jax
import jax.numpy as jnp
from jax import lax
from jax.experimental import pallas as pl
from jax.experimental.pallas import tpu as pltpu
from jax.sharding import PartitionSpec as P

HEAD_DIM = 128
TILE = 128
SPAN = 2
RUN_ROWS = 16
STATS = 6
STAT_TILE = 16
BLOCKS = 4
SCALE = 1.0 / math.sqrt(HEAD_DIM)
SCALE_LOG2 = SCALE * math.log2(math.e)
BOTH = ("ctx", "head")
NT = (((1,), (1,)), ((), ()))
TN = (((0,), (0,)), ((), ()))
NN = (((1,), (0,)), ((), ()))
VMEM_LIMIT = 32 * 1024 * 1024
VMEM_PACK = 60 * 1024 * 1024
VMEM_ALONE = 32 * 1024 * 1024
VMEM = pl.BlockSpec(memory_space=pltpu.VMEM)
SMEM = pl.BlockSpec(memory_space=pltpu.SMEM)
ANY = pl.BlockSpec(memory_space=pl.ANY)


def dot(a, b, dims):
    return lax.dot_general(a, b, dims, preferred_element_type=jnp.float32)


def kernel_call(kernel, out_shape, operands, flops, transcendentals=0):
    moved = sum(x.size * x.dtype.itemsize for x in operands)
    return pl.pallas_call(
        kernel,
        in_specs=[SMEM if x.dtype == jnp.int32 else VMEM for x in operands],
        out_specs=jax.tree.map(lambda _: VMEM, out_shape),
        out_shape=out_shape,
        compiler_params=pltpu.CompilerParams(vmem_limit_bytes=VMEM_LIMIT),
        cost_estimate=pl.CostEstimate(
            flops=flops, bytes_accessed=moved, transcendentals=transcendentals
        ),
    )(*operands)


def send(array, rule):
    n_ctx, n_head = lax.axis_size("ctx"), lax.axis_size("head")
    pairs = []
    for c in range(n_ctx):
        for h in range(n_head):
            to = rule(c, h)
            if 0 <= to[0] < n_ctx:
                pairs.append((c * n_head + h, to[0] * n_head + to[1]))
    return lax.ppermute(array, BOTH, pairs)


def in_pair(c, h):
    return (c ^ 1, h)


def even_chain(c, h):
    return (c ^ 2, h)


def odd_chain(c, h):
    return (c + 2, h) if c & 2 else (c - 2, h)


def across(c, h):
    return (c + 1, h) if c & 1 else (c - 1, h)


def forward(c, h):
    if h & 1:
        return (c ^ 1, h)
    return (c - 2, h) if c & 1 else (c + 2, h)


def offsets(pos):
    pair = 1 - 2 * lax.rem(pos, 2)
    chain = 2 - 4 * lax.rem(pos // 2, 2)
    return pair, chain, -chain, -pair


def after(value, *others):
    return lax.optimization_barrier((value,) + others)[0]


def pack_kernel(*refs):
    arrays, out_ref, sems = refs[:-2], refs[-2], refs[-1]
    rows = arrays[0].shape[0]
    copies = [
        pltpu.make_async_copy(ref, out_ref.at[n * rows:(n + 1) * rows], sems.at[n])
        for n, ref in enumerate(arrays)
    ]
    for copy in copies:
        copy.start()
    for copy in copies:
        copy.wait()


def pack(*arrays):
    rows, feat = arrays[0].shape
    count = len(arrays)
    return pl.pallas_call(
        pack_kernel,
        in_specs=[ANY] * count,
        out_specs=VMEM,
        out_shape=jax.ShapeDtypeStruct((count * rows, feat), arrays[0].dtype),
        scratch_shapes=[pltpu.SemaphoreType.DMA((count,))],
        compiler_params=pltpu.CompilerParams(vmem_limit_bytes=VMEM_PACK),
        cost_estimate=pl.CostEstimate(
            flops=0, bytes_accessed=4 * count * rows * feat, transcendentals=0
        ),
    )(*arrays)


def begin_kernel(order_ref, w_ref, g_a, g_b, out_ref, kept_ref, used, sems):
    cols = g_a.shape[1]
    copies = []
    for n in range(4):
        start = pl.multiple_of(order_ref[n] * cols, cols)
        to = used.at[n] if n < 2 else kept_ref.at[:, (n - 2) * cols:(n - 1) * cols]
        copies.append(pltpu.make_async_copy(w_ref.at[:, pl.ds(start, cols)], to, sems.at[n]))
        copies[-1].start()
    copies[0].wait()
    total = dot(used[0], g_a[...], NT)
    copies[1].wait()
    out_ref[...] = total + dot(used[1], g_b[...], NT)
    copies[2].wait()
    copies[3].wait()


def begin_project(order, out_weight, g_a, g_b):
    rows, cols = g_a.shape
    feat = out_weight.shape[0]
    return pl.pallas_call(
        begin_kernel,
        in_specs=[SMEM, ANY, VMEM, VMEM],
        out_specs=[VMEM, VMEM],
        out_shape=[
            jax.ShapeDtypeStruct((feat, rows), jnp.float32),
            jax.ShapeDtypeStruct((feat, 2 * cols), out_weight.dtype),
        ],
        scratch_shapes=[
            pltpu.VMEM((2, feat, cols), out_weight.dtype),
            pltpu.SemaphoreType.DMA((4,)),
        ],
        compiler_params=pltpu.CompilerParams(vmem_limit_bytes=VMEM_ALONE),
        cost_estimate=pl.CostEstimate(
            flops=4 * rows * cols * feat, bytes_accessed=8 * feat * cols, transcendentals=0
        ),
    )(order, out_weight, g_a, g_b)


def end_kernel(w_ref, g_a, g_b, begun, out_ref):
    cols = g_a.shape[1]
    total = begun[...] + dot(w_ref[:, :cols], g_a[...], NT)
    out_ref[...] = (total + dot(w_ref[:, cols:], g_b[...], NT)).astype(out_ref.dtype)


def end_project(weight, g_a, g_b, begun):
    rows, cols = g_a.shape
    feat = weight.shape[0]
    return kernel_call(
        end_kernel,
        jax.ShapeDtypeStruct((feat, rows), jnp.bfloat16),
        [weight, g_a, g_b, begun],
        4 * rows * cols * feat,
    )


def columns(head):
    return slice(head * HEAD_DIM, (head + 1) * HEAD_DIM)


def stat_rows(heads):
    return -(-heads * STATS // STAT_TILE) * STAT_TILE


def block_rows(n, head, rows):
    at = (head * BLOCKS + n) * rows
    return slice(at, at + rows)


def bias_row(live_flags):
    parts = [
        jnp.full((1, TILE), jnp.where(flag, 0.0, -jnp.inf).astype(jnp.float32))
        for flag in live_flags
    ]
    return jnp.concatenate(parts, axis=1)


def bias_kernel(pos_ref, mask_ref, window_ref, source_ref):
    pos = pos_ref[0]
    rows = window_ref.shape[1]
    tiles = rows // TILE
    total_tiles = mask_ref.shape[0]
    window_ref[...] = jnp.zeros_like(window_ref)
    source_ref[...] = jnp.zeros_like(source_ref)
    for n, off in enumerate((0,) + offsets(pos)):
        for b in range(tiles):
            at = slice(n * tiles + b, n * tiles + b + 1)
            column = (off + SPAN) * tiles + b
            window_ref[at, :] = bias_row(
                [mask_ref[pos * tiles + a, column] > 0 for a in range(tiles)]
            )
            flags = []
            for a in range(tiles):
                tile = (pos + off) * tiles + a
                inside = (tile >= 0) & (tile < total_tiles)
                column = (SPAN - off) * tiles + b
                flags.append(inside & (mask_ref[jnp.clip(tile, 0, total_tiles - 1), column] > 0))
            source_ref[at, :] = bias_row(flags)


def biases_of(pos, tile_mask, rows):
    count = -(-(2 * SPAN + 1) * (rows // TILE) // 8) * 8
    shape = jax.ShapeDtypeStruct((count, rows), jnp.float32)
    return kernel_call(bias_kernel, [shape, shape], [pos, tile_mask], 0)


def bias_rows(ref, which):
    tiles = ref.shape[1] // TILE
    return [[ref[n * tiles + b:n * tiles + b + 1, :] for b in range(tiles)] for n in which]


def over_keys(reduce, values):
    return reduce(values.reshape(TILE // 8, 8, values.shape[1]), axis=0)


def softmax_part(scores, biases):
    shifted = []
    top = None
    for block, rows in zip(scores, biases):
        shifted.append([])
        for b, row in enumerate(rows):
            value = block[b * TILE:(b + 1) * TILE] * SCALE_LOG2 + row
            shifted[-1].append(value)
            peak = over_keys(jnp.max, value)
            top = peak if top is None else jnp.maximum(top, peak)
    return shifted, jnp.max(top, axis=0, keepdims=True)


def weighted_values(shifted, top, values_of, keep=None):
    totals = None
    blocks = []
    for n, parts in enumerate(shifted):
        weights = []
        for value in parts:
            weight = jnp.exp2(value - top)
            weights.append(weight)
            part = over_keys(jnp.sum, weight)
            totals = part if totals is None else totals + part
        weights = jnp.concatenate(weights, axis=0)
        if keep is not None:
            keep(n, weights)
        blocks.append(weights.astype(jnp.bfloat16))
    values = jnp.concatenate([values_of(n) for n in range(len(blocks))], axis=0)
    out = dot(values, jnp.concatenate(blocks, axis=0), TN)
    return jnp.sum(totals, axis=0, keepdims=True), out


def in_order(steps, ahead_of, finish):
    ahead = ahead_of(*steps[0])
    for at, step in enumerate(steps):
        now = ahead
        if at + 1 < len(steps):
            ahead = ahead_of(*steps[at + 1])
        finish(*step, now)


def forward_kernel(which, bias_ref, *rest):
    windows, (out_ref, run_ref, kept_ref) = rest[:len(which)], rest[len(which):]
    feat, rows = out_ref.shape
    biases = bias_rows(bias_ref, which)

    def scores_of(head):
        cols = columns(head)
        q = windows[0][2 * rows:, cols]
        return [dot(w[:rows, cols], q, NT) for w in windows]

    def finish(head, scores):
        cols = columns(head)

        def values_of(n):
            return windows[n][rows:2 * rows, cols]

        def keep(n, weights):
            kept_ref[block_rows(n, head, rows), :] = weights

        shifted, top = softmax_part(scores, biases)
        totals, out = weighted_values(shifted, top, values_of, keep)
        out_ref[cols, :] = out
        at = head * RUN_ROWS
        run_ref[at:at + 8, :] = jnp.broadcast_to(top, (8, rows))
        run_ref[at + 8:at + 16, :] = jnp.broadcast_to(totals, (8, rows))

    in_order([(head,) for head in range(feat // HEAD_DIM)], scores_of, finish)


def forward_part(bias, own, which, windows):
    rows, feat = own.shape[0] // 3, own.shape[1]
    heads = feat // HEAD_DIM
    return kernel_call(
        functools.partial(forward_kernel, which),
        [
            jax.ShapeDtypeStruct((feat, rows), jnp.float32),
            jax.ShapeDtypeStruct((heads * RUN_ROWS, rows), jnp.float32),
            jax.ShapeDtypeStruct((len(which) * feat // HEAD_DIM * rows, rows), jnp.float32),
        ],
        [bias, own, *windows],
        4 * len(which) * rows * rows * feat,
        len(which) * rows * rows * heads,
    )


def statistics_kernel(
    which, bias_ref, own_ref, w_ref, out_in, run_in, d_ref, stats_ref, packed_ref
):
    feat, rows = d_ref.shape
    biases = bias_rows(bias_ref, [which])

    def scores_of(head):
        cols = columns(head)
        return [dot(w_ref[:rows, cols], own_ref[2 * rows:, cols], NT)]

    def finish(head, scores):
        cols = columns(head)

        def values_of(n):
            return w_ref[rows:, cols]

        at = head * RUN_ROWS
        top_before, totals_before = run_in[at:at + 1, :], run_in[at + 8:at + 9, :]
        shifted, top = softmax_part(scores, biases)
        top = jnp.maximum(top, top_before)
        totals, out = weighted_values(shifted, top, values_of)
        shrink = jnp.exp2(top_before - top)
        totals = totals + totals_before * shrink
        out = out + out_in[cols, :] * shrink
        attn_out = (out / totals).astype(jnp.bfloat16).astype(jnp.float32)
        delta = jnp.sum(d_ref[cols, :].astype(jnp.float32) * attn_out, axis=0, keepdims=True)
        place = head * STATS
        for stat in (top + jnp.log2(totals), delta):
            for _ in range(3):
                piece = stat.astype(jnp.bfloat16).astype(jnp.float32)
                all_stats[0] = jnp.where(row == place, piece, all_stats[0])
                stat = stat - piece
                place += 1
        packed_ref[cols, :] = d_ref[cols, :]

    row = lax.broadcasted_iota(jnp.int32, stats_ref.shape, 0)
    all_stats = [jnp.zeros(stats_ref.shape, jnp.float32)]
    in_order([(head,) for head in range(feat // HEAD_DIM)], scores_of, finish)
    stats_ref[...] = all_stats[0].astype(jnp.bfloat16)
    packed_ref[feat:, :] = all_stats[0].astype(jnp.bfloat16)


def statistics(bias, own, which, window, out, run, d_out_t):
    feat, rows = d_out_t.shape
    heads = feat // HEAD_DIM
    return kernel_call(
        functools.partial(statistics_kernel, which),
        [
            jax.ShapeDtypeStruct((stat_rows(heads), rows), jnp.bfloat16),
            jax.ShapeDtypeStruct((feat + stat_rows(heads), rows), jnp.bfloat16),
        ],
        [bias, own, window, out, run, d_out_t],
        4 * rows * rows * feat,
        rows * rows * heads,
    )


def statistics_of(ref, start, head):
    stats = ref[start:, :].astype(jnp.float32)
    rows = [stats[head * STATS + n:head * STATS + n + 1] for n in range(STATS)]
    return rows[0] + rows[1] + rows[2], rows[3] + rows[4] + rows[5]


def block_grads(scores, dprobs, bias_rows, lse, delta):
    probs = jnp.concatenate(
        [
            jnp.exp2(scores[b * TILE:(b + 1) * TILE] * SCALE_LOG2 + (row - lse))
            for b, row in enumerate(bias_rows)
        ],
        axis=0,
    )
    dscores = probs * (dprobs - delta)
    return probs.astype(jnp.bfloat16), dscores.astype(jnp.bfloat16)


def query_kernel(which, bias_ref, own_ref, *rest):
    windows, rest = (own_ref,) + rest[:BLOCKS], rest[BLOCKS:]
    d_ref, s_ref, run_ref, kept_ref, q_last, d_last, *outs = rest
    dq_ref, dk_ref, dv_ref, scores_ref, dprobs_ref = outs
    rows, feat = dq_ref.shape
    last_bias = bias_rows(bias_ref, which[BLOCKS:])[0]

    def products(head):
        cols = columns(head)
        keys, values = own_ref[:rows, cols], own_ref[rows:2 * rows, cols]
        queries = own_ref[2 * rows:, cols]
        for n in range(BLOCKS):
            others = q_last[:, cols] if n == BLOCKS - 1 else windows[n + 1][2 * rows:, cols]
            scores_ref[block_rows(n, head, rows), :] = dot(keys, others, NT)
        dprobs_ref[head * rows:(head + 1) * rows, :] = dot(values, d_last[cols, :], NN)
        scores = dot(windows[BLOCKS][:rows, cols], queries, NT)
        return scores, [dot(w[rows:2 * rows, cols], d_ref[cols, :], NN) for w in windows]

    def finish(head, now):
        cols = columns(head)
        scores, dprobs = now
        lse, delta = statistics_of(s_ref, 0, head)
        at = head * RUN_ROWS
        factor = jnp.exp2(run_ref[at:at + 1, :] - lse)
        dscores = []
        for n in range(BLOCKS):
            probs = kept_ref[block_rows(n, head, rows), :] * factor
            dscores.append((probs * (dprobs[n] - delta)).astype(jnp.bfloat16))
            if n == 0:
                dv_ref[:, cols] = dot(probs.astype(jnp.bfloat16), d_ref[cols, :], NT)
        dk_ref[:, cols] = dot(dscores[0], own_ref[2 * rows:, cols], NN)
        dscores.append(block_grads(scores, dprobs[BLOCKS], last_bias, lse, delta)[1])
        keys = jnp.concatenate([w[:rows, cols] for w in windows], axis=0)
        dq = dot(keys, jnp.concatenate(dscores, axis=0), TN)
        dq_ref[:, cols] = jnp.transpose(dq * SCALE).astype(dq_ref.dtype)

    in_order([(head,) for head in range(feat // HEAD_DIM)], products, finish)


def query_side(bias, own, which, windows, d_out_t, stats, run, kept, q_last, d_last):
    feat, rows = d_out_t.shape
    heads = feat // HEAD_DIM
    total = jax.ShapeDtypeStruct((rows, feat), jnp.float32)
    return kernel_call(
        functools.partial(query_kernel, which),
        [
            jax.ShapeDtypeStruct((rows, feat), jnp.bfloat16),
            total,
            total,
            jax.ShapeDtypeStruct((heads * BLOCKS * rows, rows), jnp.float32),
            jax.ShapeDtypeStruct((heads * rows, rows), jnp.float32),
        ],
        [bias, own, *windows, d_out_t, stats, run, kept, q_last, d_last],
        36 * rows * rows * feat,
        rows * rows * heads,
    )


def key_kernel(which, bias_ref, own_ref, *rest):
    sources = [rest[3 * n:3 * n + 3] for n in range(BLOCKS)]
    scores_ref, dprobs_ref, dk_in, dv_in, dk_out, dv_out, dk_ref, dv_ref, sems = rest[3 * BLOCKS:]
    copies = []
    rows, feat = dk_in.shape
    biases = bias_rows(bias_ref, which)

    def products(head):
        cols = columns(head)
        values = own_ref[rows:2 * rows, cols]
        dprobs = [dot(values, sources[n][1][cols, :], NN) for n in range(BLOCKS - 1)]
        return dprobs + [dprobs_ref[head * rows:(head + 1) * rows, :]]

    def finish(head, dprobs):
        cols = columns(head)
        blocks = []
        for n, (_, _, s_ref) in enumerate(sources):
            start = feat if s_ref.shape[0] > feat else 0
            scores = scores_ref[block_rows(n, head, rows), :]
            blocks.append(
                block_grads(scores, dprobs[n], biases[n], *statistics_of(s_ref, start, head))
            )
        probs, dscores = (jnp.concatenate(parts, axis=1) for parts in zip(*blocks))
        queries = jnp.concatenate([q[q.shape[0] - rows:, cols] for q, _, _ in sources], axis=0)
        grads = jnp.concatenate([d[cols, :] for _, d, _ in sources], axis=1)
        dk = dk_in[:, cols] + dot(dscores, queries, NN)
        dv = dv_in[:, cols] + dot(probs, grads, NT)
        dk_ref[:, cols] = (dk * SCALE).astype(dk_ref.dtype)
        dv_ref[:, cols] = dv.astype(dv_ref.dtype)
        for which_out, (from_ref, to_ref) in enumerate(((dk_ref, dk_out), (dv_ref, dv_out))):
            copies.append(
                pltpu.make_async_copy(
                    from_ref.at[:, cols], to_ref.at[:, cols], sems.at[2 * head + which_out]
                )
            )
            copies[-1].start()

    in_order([(head,) for head in range(feat // HEAD_DIM)], products, finish)
    for copy in copies:
        copy.wait()


def key_side(bias, own, sources, scores, dprobs, begun):
    rows, feat = begun[0].shape
    operands = [bias, own]
    for _, q, d, s in sources:
        operands += [q, d, s]
    operands += [scores, dprobs, *begun]
    return pl.pallas_call(
        functools.partial(key_kernel, [source[0] for source in sources]),
        in_specs=[VMEM] * len(operands),
        out_specs=[ANY] * 2,
        out_shape=[jax.ShapeDtypeStruct((rows, feat), jnp.bfloat16)] * 2,
        scratch_shapes=[
            pltpu.VMEM((rows, feat), jnp.bfloat16),
            pltpu.VMEM((rows, feat), jnp.bfloat16),
            pltpu.SemaphoreType.DMA((2 * feat // HEAD_DIM,)),
        ],
        compiler_params=pltpu.CompilerParams(vmem_limit_bytes=VMEM_LIMIT),
        cost_estimate=pl.CostEstimate(
            flops=26 * rows * rows * feat,
            bytes_accessed=sum(x.size * x.dtype.itemsize for x in operands),
            transcendentals=BLOCKS * rows * rows * feat // HEAD_DIM,
        ),
    )(*operands)


def local(queries, keys, values, out_weight, reward_grad, tile_mask):
    rows = queries.shape[0]
    ctx = lax.axis_index("ctx").astype(jnp.int32)
    head = lax.axis_index("head").astype(jnp.int32)
    pos = ctx.reshape(1)

    def second_step(x, a, b):
        a_is_held = (ctx % 2 == 0) == (ctx // 2 % 2 == 0)
        return jnp.where(head % 2 == 1, jnp.where(a_is_held, a, b), x)

    far = send(reward_grad, lambda c, h: (c, h ^ 2))
    kvq = pack(keys, values, queries)
    kvq_b = send(kvq, odd_chain)
    kvq_a = send(kvq, even_chain)
    kvq_x = send(kvq, in_pair)
    near = send(after(reward_grad, kvq), lambda c, h: (c, h ^ 1))
    order = jnp.stack([head, head ^ 1, head ^ 2, head ^ 3])
    own_bias, other_bias = biases_of(pos, tile_mask, rows)
    near = after(near, own_bias, other_bias)
    begun, kept = begin_project(order, out_weight, reward_grad, near)
    far = after(far, begun)
    far_near = send(far, lambda c, h: (c, h ^ 1))
    second = second_step(kvq_x, kvq_a, kvq_b)
    kv_g = send(second[:2 * rows], forward)
    d_out_t = end_project(kept, far, far_near, after(begun, second))
    out, run, kept_weights = forward_part(
        own_bias, after(kvq, d_out_t), [0, 1, 2, 3], [kvq_x, kvq_a, kvq_b]
    )
    stats, packed = statistics(own_bias, kvq, 4, kv_g, out, run, d_out_t)
    q_g = send(after(second[2 * rows:], out), forward)
    d_g = send(d_out_t, across)
    p_b = send(packed, odd_chain)
    p_a = send(packed, even_chain)
    p_x = send(packed, in_pair)
    s_g = send(stats, across)
    grad_queries, *begun_keys, scores, dprobs = query_side(
        own_bias, kvq, [0, 1, 2, 3, 4], [kvq_x, kvq_a, kvq_b, kv_g], d_out_t,
        stats, run, kept_weights, q_g, d_g,
    )
    grad_keys, grad_values = key_side(
        other_bias,
        kvq,
        [
            (1, kvq_x, p_x, p_x),
            (2, kvq_a, p_a, p_a),
            (3, kvq_b, p_b, p_b),
            (4, q_g, d_g, s_g),
        ],
        scores,
        dprobs,
        begun_keys,
    )
    return (grad_queries, grad_keys, grad_values)


def solution(mesh):
    placed = (
        P("ctx", "head"),
        P("ctx", "head"),
        P("ctx", "head"),
        P("head", None),
        P("ctx", "head"),
        P(),
    )
    return jax.shard_map(
        local,
        mesh=mesh,
        in_specs=placed,
        out_specs=(P("ctx", "head"), P("ctx", "head"), P("ctx", "head")),
        check_vma=False,
    )
```

```python
import functools
import math

import jax
import jax.numpy as jnp
from jax import lax
from jax.experimental import pallas as pl
from jax.experimental.pallas import tpu as pltpu
from jax.sharding import PartitionSpec as P

HEAD_DIM = 128
TILE = 128
SPAN = 2
RUN_ROWS = 16
STATS = 6
STAT_TILE = 16
BLOCKS = 4
SCALE = 1.0 / math.sqrt(HEAD_DIM)
SCALE_LOG2 = SCALE * math.log2(math.e)
BOTH = ("ctx", "head")
NT = (((1,), (1,)), ((), ()))
TN = (((0,), (0,)), ((), ()))
NN = (((1,), (0,)), ((), ()))
VMEM_LIMIT = 32 * 1024 * 1024
VMEM_PACK = 60 * 1024 * 1024
VMEM_ALONE = 32 * 1024 * 1024
VMEM = pl.BlockSpec(memory_space=pltpu.VMEM)
SMEM = pl.BlockSpec(memory_space=pltpu.SMEM)
ANY = pl.BlockSpec(memory_space=pl.ANY)


def dot(a, b, dims):
    return lax.dot_general(a, b, dims, preferred_element_type=jnp.float32)


def kernel_call(kernel, out_shape, operands, flops, transcendentals=0):
    moved = sum(x.size * x.dtype.itemsize for x in operands)
    return pl.pallas_call(
        kernel,
        in_specs=[SMEM if x.dtype == jnp.int32 else VMEM for x in operands],
        out_specs=jax.tree.map(lambda _: VMEM, out_shape),
        out_shape=out_shape,
        compiler_params=pltpu.CompilerParams(vmem_limit_bytes=VMEM_LIMIT),
        cost_estimate=pl.CostEstimate(
            flops=flops, bytes_accessed=moved, transcendentals=transcendentals
        ),
    )(*operands)


def send(array, rule):
    n_ctx, n_head = lax.axis_size("ctx"), lax.axis_size("head")
    pairs = []
    for c in range(n_ctx):
        for h in range(n_head):
            to = rule(c, h)
            if 0 <= to[0] < n_ctx:
                pairs.append((c * n_head + h, to[0] * n_head + to[1]))
    return lax.ppermute(array, BOTH, pairs)


def in_pair(c, h):
    return (c ^ 1, h)


def even_chain(c, h):
    return (c ^ 2, h)


def odd_chain(c, h):
    return (c + 2, h) if c & 2 else (c - 2, h)


def across(c, h):
    return (c + 1, h) if c & 1 else (c - 1, h)


def forward(c, h):
    if h & 1:
        return (c ^ 1, h)
    return (c - 2, h) if c & 1 else (c + 2, h)


def offsets(pos):
    pair = 1 - 2 * lax.rem(pos, 2)
    chain = 2 - 4 * lax.rem(pos // 2, 2)
    return pair, chain, -chain, -pair


def after(value, *others):
    return lax.optimization_barrier((value,) + others)[0]


def pack_kernel(*refs):
    arrays, out_ref, sems = refs[:-2], refs[-2], refs[-1]
    rows = arrays[0].shape[0]
    copies = [
        pltpu.make_async_copy(ref, out_ref.at[n * rows:(n + 1) * rows], sems.at[n])
        for n, ref in enumerate(arrays)
    ]
    for copy in copies:
        copy.start()
    for copy in copies:
        copy.wait()


def pack(*arrays):
    rows, feat = arrays[0].shape
    count = len(arrays)
    return pl.pallas_call(
        pack_kernel,
        in_specs=[ANY] * count,
        out_specs=VMEM,
        out_shape=jax.ShapeDtypeStruct((count * rows, feat), arrays[0].dtype),
        scratch_shapes=[pltpu.SemaphoreType.DMA((count,))],
        compiler_params=pltpu.CompilerParams(vmem_limit_bytes=VMEM_PACK),
        cost_estimate=pl.CostEstimate(
            flops=0, bytes_accessed=4 * count * rows * feat, transcendentals=0
        ),
    )(*arrays)


def begin_kernel(order_ref, w_ref, g_a, g_b, out_ref, kept_ref, used, sems):
    cols = g_a.shape[1]
    copies = []
    for n in range(4):
        start = pl.multiple_of(order_ref[n] * cols, cols)
        to = used.at[n] if n < 2 else kept_ref.at[:, (n - 2) * cols:(n - 1) * cols]
        copies.append(pltpu.make_async_copy(w_ref.at[:, pl.ds(start, cols)], to, sems.at[n]))
        copies[-1].start()
    copies[0].wait()
    total = dot(used[0], g_a[...], NT)
    copies[1].wait()
    out_ref[...] = total + dot(used[1], g_b[...], NT)
    copies[2].wait()
    copies[3].wait()


def begin_project(order, out_weight, g_a, g_b):
    rows, cols = g_a.shape
    feat = out_weight.shape[0]
    return pl.pallas_call(
        begin_kernel,
        in_specs=[SMEM, ANY, VMEM, VMEM],
        out_specs=[VMEM, VMEM],
        out_shape=[
            jax.ShapeDtypeStruct((feat, rows), jnp.float32),
            jax.ShapeDtypeStruct((feat, 2 * cols), out_weight.dtype),
        ],
        scratch_shapes=[
            pltpu.VMEM((2, feat, cols), out_weight.dtype),
            pltpu.SemaphoreType.DMA((4,)),
        ],
        compiler_params=pltpu.CompilerParams(vmem_limit_bytes=VMEM_ALONE),
        cost_estimate=pl.CostEstimate(
            flops=4 * rows * cols * feat, bytes_accessed=8 * feat * cols, transcendentals=0
        ),
    )(order, out_weight, g_a, g_b)


def end_kernel(w_ref, g_a, g_b, begun, out_ref):
    cols = g_a.shape[1]
    total = begun[...] + dot(w_ref[:, :cols], g_a[...], NT)
    out_ref[...] = (total + dot(w_ref[:, cols:], g_b[...], NT)).astype(out_ref.dtype)


def end_project(weight, g_a, g_b, begun):
    rows, cols = g_a.shape
    feat = weight.shape[0]
    return kernel_call(
        end_kernel,
        jax.ShapeDtypeStruct((feat, rows), jnp.bfloat16),
        [weight, g_a, g_b, begun],
        4 * rows * cols * feat,
    )


def columns(head):
    return slice(head * HEAD_DIM, (head + 1) * HEAD_DIM)


def stat_rows(heads):
    return -(-heads * STATS // STAT_TILE) * STAT_TILE


def block_rows(n, head, rows):
    at = (head * BLOCKS + n) * rows
    return slice(at, at + rows)


def bias_row(live_flags):
    parts = [
        jnp.full((1, TILE), jnp.where(flag, 0.0, -jnp.inf).astype(jnp.float32))
        for flag in live_flags
    ]
    return jnp.concatenate(parts, axis=1)


def bias_kernel(pos_ref, mask_ref, window_ref, source_ref):
    pos = pos_ref[0]
    rows = window_ref.shape[1]
    tiles = rows // TILE
    total_tiles = mask_ref.shape[0]
    window_ref[...] = jnp.zeros_like(window_ref)
    source_ref[...] = jnp.zeros_like(source_ref)
    for n, off in enumerate((0,) + offsets(pos)):
        for b in range(tiles):
            at = slice(n * tiles + b, n * tiles + b + 1)
            column = (off + SPAN) * tiles + b
            window_ref[at, :] = bias_row(
                [mask_ref[pos * tiles + a, column] > 0 for a in range(tiles)]
            )
            flags = []
            for a in range(tiles):
                tile = (pos + off) * tiles + a
                inside = (tile >= 0) & (tile < total_tiles)
                column = (SPAN - off) * tiles + b
                flags.append(inside & (mask_ref[jnp.clip(tile, 0, total_tiles - 1), column] > 0))
            source_ref[at, :] = bias_row(flags)


def biases_of(pos, tile_mask, rows):
    count = -(-(2 * SPAN + 1) * (rows // TILE) // 8) * 8
    shape = jax.ShapeDtypeStruct((count, rows), jnp.float32)
    return kernel_call(bias_kernel, [shape, shape], [pos, tile_mask], 0)


def bias_rows(ref, which):
    tiles = ref.shape[1] // TILE
    return [[ref[n * tiles + b:n * tiles + b + 1, :] for b in range(tiles)] for n in which]


def over_keys(reduce, values):
    return reduce(values.reshape(TILE // 8, 8, values.shape[1]), axis=0)


def softmax_part(scores, biases):
    shifted = []
    top = None
    for block, rows in zip(scores, biases):
        shifted.append([])
        for b, row in enumerate(rows):
            value = block[b * TILE:(b + 1) * TILE] * SCALE_LOG2 + row
            shifted[-1].append(value)
            peak = over_keys(jnp.max, value)
            top = peak if top is None else jnp.maximum(top, peak)
    return shifted, jnp.max(top, axis=0, keepdims=True)


def weighted_values(shifted, top, values_of, keep=None):
    totals = None
    blocks = []
    for n, parts in enumerate(shifted):
        weights = []
        for value in parts:
            weight = jnp.exp2(value - top)
            weights.append(weight)
            part = over_keys(jnp.sum, weight)
            totals = part if totals is None else totals + part
        weights = jnp.concatenate(weights, axis=0)
        if keep is not None:
            keep(n, weights)
        blocks.append(weights.astype(jnp.bfloat16))
    values = jnp.concatenate([values_of(n) for n in range(len(blocks))], axis=0)
    out = dot(values, jnp.concatenate(blocks, axis=0), TN)
    return jnp.sum(totals, axis=0, keepdims=True), out


def in_order(steps, ahead_of, finish):
    ahead = ahead_of(*steps[0])
    for at, step in enumerate(steps):
        now = ahead
        if at + 1 < len(steps):
            ahead = ahead_of(*steps[at + 1])
        finish(*step, now)


def forward_kernel(which, bias_ref, *rest):
    windows, (out_ref, run_ref, kept_ref) = rest[:len(which)], rest[len(which):]
    feat, rows = out_ref.shape
    biases = bias_rows(bias_ref, which)

    def scores_of(head):
        cols = columns(head)
        q = windows[0][2 * rows:, cols]
        return [dot(w[:rows, cols], q, NT) for w in windows]

    def finish(head, scores):
        cols = columns(head)

        def values_of(n):
            return windows[n][rows:2 * rows, cols]

        def keep(n, weights):
            kept_ref[block_rows(n, head, rows), :] = weights

        shifted, top = softmax_part(scores, biases)
        totals, out = weighted_values(shifted, top, values_of, keep)
        out_ref[cols, :] = out
        at = head * RUN_ROWS
        run_ref[at:at + 8, :] = jnp.broadcast_to(top, (8, rows))
        run_ref[at + 8:at + 16, :] = jnp.broadcast_to(totals, (8, rows))

    in_order([(head,) for head in range(feat // HEAD_DIM)], scores_of, finish)


def forward_part(bias, own, which, windows):
    rows, feat = own.shape[0] // 3, own.shape[1]
    heads = feat // HEAD_DIM
    return kernel_call(
        functools.partial(forward_kernel, which),
        [
            jax.ShapeDtypeStruct((feat, rows), jnp.float32),
            jax.ShapeDtypeStruct((heads * RUN_ROWS, rows), jnp.float32),
            jax.ShapeDtypeStruct((len(which) * feat // HEAD_DIM * rows, rows), jnp.float32),
        ],
        [bias, own, *windows],
        4 * len(which) * rows * rows * feat,
        len(which) * rows * rows * heads,
    )


def statistics_kernel(
    which, bias_ref, own_ref, w_ref, out_in, run_in, d_ref, stats_ref, packed_ref
):
    feat, rows = d_ref.shape
    biases = bias_rows(bias_ref, [which])

    def scores_of(head):
        cols = columns(head)
        return [dot(w_ref[:rows, cols], own_ref[2 * rows:, cols], NT)]

    def finish(head, scores):
        cols = columns(head)

        def values_of(n):
            return w_ref[rows:, cols]

        at = head * RUN_ROWS
        top_before, totals_before = run_in[at:at + 1, :], run_in[at + 8:at + 9, :]
        shifted, top = softmax_part(scores, biases)
        top = jnp.maximum(top, top_before)
        totals, out = weighted_values(shifted, top, values_of)
        shrink = jnp.exp2(top_before - top)
        totals = totals + totals_before * shrink
        out = out + out_in[cols, :] * shrink
        attn_out = (out / totals).astype(jnp.bfloat16).astype(jnp.float32)
        delta = jnp.sum(d_ref[cols, :].astype(jnp.float32) * attn_out, axis=0, keepdims=True)
        place = head * STATS
        for stat in (top + jnp.log2(totals), delta):
            for _ in range(3):
                piece = stat.astype(jnp.bfloat16).astype(jnp.float32)
                all_stats[0] = jnp.where(row == place, piece, all_stats[0])
                stat = stat - piece
                place += 1
        packed_ref[cols, :] = d_ref[cols, :]

    row = lax.broadcasted_iota(jnp.int32, stats_ref.shape, 0)
    all_stats = [jnp.zeros(stats_ref.shape, jnp.float32)]
    in_order([(head,) for head in range(feat // HEAD_DIM)], scores_of, finish)
    stats_ref[...] = all_stats[0].astype(jnp.bfloat16)
    packed_ref[feat:, :] = all_stats[0].astype(jnp.bfloat16)


def statistics(bias, own, which, window, out, run, d_out_t):
    feat, rows = d_out_t.shape
    heads = feat // HEAD_DIM
    return kernel_call(
        functools.partial(statistics_kernel, which),
        [
            jax.ShapeDtypeStruct((stat_rows(heads), rows), jnp.bfloat16),
            jax.ShapeDtypeStruct((feat + stat_rows(heads), rows), jnp.bfloat16),
        ],
        [bias, own, window, out, run, d_out_t],
        4 * rows * rows * feat,
        rows * rows * heads,
    )


def statistics_of(ref, start, head):
    stats = ref[start:, :].astype(jnp.float32)
    rows = [stats[head * STATS + n:head * STATS + n + 1] for n in range(STATS)]
    return rows[0] + rows[1] + rows[2], rows[3] + rows[4] + rows[5]


def block_grads(scores, dprobs, bias_rows, lse, delta):
    probs = jnp.concatenate(
        [
            jnp.exp2(scores[b * TILE:(b + 1) * TILE] * SCALE_LOG2 + (row - lse))
            for b, row in enumerate(bias_rows)
        ],
        axis=0,
    )
    dscores = probs * (dprobs - delta)
    return probs.astype(jnp.bfloat16), dscores.astype(jnp.bfloat16)


def query_kernel(which, bias_ref, own_ref, *rest):
    windows, rest = (own_ref,) + rest[:BLOCKS], rest[BLOCKS:]
    d_ref, s_ref, run_ref, kept_ref, q_last, d_last, *outs = rest
    dq_ref, dk_ref, dv_ref, scores_ref, dprobs_ref = outs
    rows, feat = dq_ref.shape
    last_bias = bias_rows(bias_ref, which[BLOCKS:])[0]

    def products(head):
        cols = columns(head)
        keys, values = own_ref[:rows, cols], own_ref[rows:2 * rows, cols]
        queries = own_ref[2 * rows:, cols]
        for n in range(BLOCKS):
            others = q_last[:, cols] if n == BLOCKS - 1 else windows[n + 1][2 * rows:, cols]
            scores_ref[block_rows(n, head, rows), :] = dot(keys, others, NT)
        dprobs_ref[head * rows:(head + 1) * rows, :] = dot(values, d_last[cols, :], NN)
        scores = dot(windows[BLOCKS][:rows, cols], queries, NT)
        return scores, [dot(w[rows:2 * rows, cols], d_ref[cols, :], NN) for w in windows]

    def finish(head, now):
        cols = columns(head)
        scores, dprobs = now
        lse, delta = statistics_of(s_ref, 0, head)
        at = head * RUN_ROWS
        factor = jnp.exp2(run_ref[at:at + 1, :] - lse)
        dscores = []
        for n in range(BLOCKS):
            probs = kept_ref[block_rows(n, head, rows), :] * factor
            dscores.append((probs * (dprobs[n] - delta)).astype(jnp.bfloat16))
            if n == 0:
                dv_ref[:, cols] = dot(probs.astype(jnp.bfloat16), d_ref[cols, :], NT)
        dk_ref[:, cols] = dot(dscores[0], own_ref[2 * rows:, cols], NN)
        dscores.append(block_grads(scores, dprobs[BLOCKS], last_bias, lse, delta)[1])
        keys = jnp.concatenate([w[:rows, cols] for w in windows], axis=0)
        dq = dot(keys, jnp.concatenate(dscores, axis=0), TN)
        dq_ref[:, cols] = jnp.transpose(dq * SCALE).astype(dq_ref.dtype)

    in_order([(head,) for head in range(feat // HEAD_DIM)], products, finish)


def query_side(bias, own, which, windows, d_out_t, stats, run, kept, q_last, d_last):
    feat, rows = d_out_t.shape
    heads = feat // HEAD_DIM
    total = jax.ShapeDtypeStruct((rows, feat), jnp.float32)
    return kernel_call(
        functools.partial(query_kernel, which),
        [
            jax.ShapeDtypeStruct((rows, feat), jnp.bfloat16),
            total,
            total,
            jax.ShapeDtypeStruct((heads * BLOCKS * rows, rows), jnp.float32),
            jax.ShapeDtypeStruct((heads * rows, rows), jnp.float32),
        ],
        [bias, own, *windows, d_out_t, stats, run, kept, q_last, d_last],
        36 * rows * rows * feat,
        rows * rows * heads,
    )


def key_kernel(which, bias_ref, own_ref, *rest):
    sources = [rest[3 * n:3 * n + 3] for n in range(BLOCKS)]
    scores_ref, dprobs_ref, dk_in, dv_in, dk_out, dv_out, dk_ref, dv_ref, sems = rest[3 * BLOCKS:]
    copies = []
    rows, feat = dk_in.shape
    biases = bias_rows(bias_ref, which)

    def products(head):
        cols = columns(head)
        values = own_ref[rows:2 * rows, cols]
        dprobs = [dot(values, sources[n][1][cols, :], NN) for n in range(BLOCKS - 1)]
        return dprobs + [dprobs_ref[head * rows:(head + 1) * rows, :]]

    def finish(head, dprobs):
        cols = columns(head)
        blocks = []
        for n, (_, _, s_ref) in enumerate(sources):
            start = feat if s_ref.shape[0] > feat else 0
            scores = scores_ref[block_rows(n, head, rows), :]
            blocks.append(
                block_grads(scores, dprobs[n], biases[n], *statistics_of(s_ref, start, head))
            )
        probs, dscores = (jnp.concatenate(parts, axis=1) for parts in zip(*blocks))
        queries = jnp.concatenate([q[q.shape[0] - rows:, cols] for q, _, _ in sources], axis=0)
        grads = jnp.concatenate([d[cols, :] for _, d, _ in sources], axis=1)
        dk = dk_in[:, cols] + dot(dscores, queries, NN)
        dv = dv_in[:, cols] + dot(probs, grads, NT)
        dk_ref[:, cols] = (dk * SCALE).astype(dk_ref.dtype)
        dv_ref[:, cols] = dv.astype(dv_ref.dtype)
        for which_out, (from_ref, to_ref) in enumerate(((dk_ref, dk_out), (dv_ref, dv_out))):
            copies.append(
                pltpu.make_async_copy(
                    from_ref.at[:, cols], to_ref.at[:, cols], sems.at[2 * head + which_out]
                )
            )
            copies[-1].start()

    in_order([(head,) for head in range(feat // HEAD_DIM)], products, finish)
    for copy in copies:
        copy.wait()


def key_side(bias, own, sources, scores, dprobs, begun):
    rows, feat = begun[0].shape
    operands = [bias, own]
    for _, q, d, s in sources:
        operands += [q, d, s]
    operands += [scores, dprobs, *begun]
    return pl.pallas_call(
        functools.partial(key_kernel, [source[0] for source in sources]),
        in_specs=[VMEM] * len(operands),
        out_specs=[ANY] * 2,
        out_shape=[jax.ShapeDtypeStruct((rows, feat), jnp.bfloat16)] * 2,
        scratch_shapes=[
            pltpu.VMEM((rows, feat), jnp.bfloat16),
            pltpu.VMEM((rows, feat), jnp.bfloat16),
            pltpu.SemaphoreType.DMA((2 * feat // HEAD_DIM,)),
        ],
        compiler_params=pltpu.CompilerParams(vmem_limit_bytes=VMEM_LIMIT),
        cost_estimate=pl.CostEstimate(
            flops=26 * rows * rows * feat,
            bytes_accessed=sum(x.size * x.dtype.itemsize for x in operands),
            transcendentals=BLOCKS * rows * rows * feat // HEAD_DIM,
        ),
    )(*operands)


def local(queries, keys, values, out_weight, reward_grad, tile_mask):
    rows = queries.shape[0]
    ctx = lax.axis_index("ctx").astype(jnp.int32)
    head = lax.axis_index("head").astype(jnp.int32)
    pos = ctx.reshape(1)

    def second_step(x, a, b):
        a_is_held = (ctx % 2 == 0) == (ctx // 2 % 2 == 0)
        return jnp.where(head % 2 == 1, jnp.where(a_is_held, a, b), x)

    far = send(reward_grad, lambda c, h: (c, h ^ 2))
    kvq = pack(keys, values, queries)
    kvq_b = send(kvq, odd_chain)
    kvq_a = send(kvq, even_chain)
    kvq_x = send(kvq, in_pair)
    near = send(after(reward_grad, kvq), lambda c, h: (c, h ^ 1))
    order = jnp.stack([head, head ^ 1, head ^ 2, head ^ 3])
    own_bias, other_bias = biases_of(pos, tile_mask, rows)
    near = after(near, own_bias, other_bias)
    begun, kept = begin_project(order, out_weight, reward_grad, near)
    far = after(far, begun)
    far_near = send(far, lambda c, h: (c, h ^ 1))
    second = second_step(kvq_x, kvq_a, kvq_b)
    kv_g = send(second[:2 * rows], forward)
    d_out_t = end_project(kept, far, far_near, after(begun, second))
    out, run, kept_weights = forward_part(
        own_bias, kvq, [0, 1, 2, 3], [kvq_x, kvq_a, kvq_b]
    )
    stats, packed = statistics(own_bias, kvq, 4, kv_g, out, run, d_out_t)
    q_g = send(second[2 * rows:], forward)
    d_g = send(d_out_t, across)
    p_b = send(packed, odd_chain)
    p_a = send(packed, even_chain)
    p_x = send(packed, in_pair)
    s_g = send(stats, across)
    grad_queries, *begun_keys, scores, dprobs = query_side(
        own_bias, kvq, [0, 1, 2, 3, 4], [kvq_x, kvq_a, kvq_b, kv_g], d_out_t,
        stats, run, kept_weights, q_g, d_g,
    )
    grad_keys, grad_values = key_side(
        other_bias,
        kvq,
        [
            (1, kvq_x, p_x, p_x),
            (2, kvq_a, p_a, p_a),
            (3, kvq_b, p_b, p_b),
            (4, q_g, d_g, s_g),
        ],
        scores,
        dprobs,
        begun_keys,
    )
    return (grad_queries, grad_keys, grad_values)


def solution(mesh):
    placed = (
        P("ctx", "head"),
        P("ctx", "head"),
        P("ctx", "head"),
        P("head", None),
        P("ctx", "head"),
        P(),
    )
    return jax.shard_map(
        local,
        mesh=mesh,
        in_specs=placed,
        out_specs=(P("ctx", "head"), P("ctx", "head"), P("ctx", "head")),
        check_vma=False,
    )
```

```python
import functools
import math

import jax
import jax.numpy as jnp
from jax import lax
from jax.experimental import pallas as pl
from jax.experimental.pallas import tpu as pltpu
from jax.sharding import PartitionSpec as P

HEAD_DIM = 128
TILE = 128
SPAN = 2
RUN_ROWS = 16
STATS = 6
STAT_TILE = 16
BLOCKS = 4
SCALE = 1.0 / math.sqrt(HEAD_DIM)
SCALE_LOG2 = SCALE * math.log2(math.e)
BOTH = ("ctx", "head")
NT = (((1,), (1,)), ((), ()))
TN = (((0,), (0,)), ((), ()))
NN = (((1,), (0,)), ((), ()))
VMEM_LIMIT = 32 * 1024 * 1024
VMEM_PACK = 60 * 1024 * 1024
VMEM_ALONE = 32 * 1024 * 1024
VMEM = pl.BlockSpec(memory_space=pltpu.VMEM)
SMEM = pl.BlockSpec(memory_space=pltpu.SMEM)
ANY = pl.BlockSpec(memory_space=pl.ANY)


def dot(a, b, dims):
    return lax.dot_general(a, b, dims, preferred_element_type=jnp.float32)


def kernel_call(kernel, out_shape, operands, flops, transcendentals=0):
    moved = sum(x.size * x.dtype.itemsize for x in operands)
    return pl.pallas_call(
        kernel,
        in_specs=[SMEM if x.dtype == jnp.int32 else VMEM for x in operands],
        out_specs=jax.tree.map(lambda _: VMEM, out_shape),
        out_shape=out_shape,
        compiler_params=pltpu.CompilerParams(vmem_limit_bytes=VMEM_LIMIT),
        cost_estimate=pl.CostEstimate(
            flops=flops, bytes_accessed=moved, transcendentals=transcendentals
        ),
    )(*operands)


def send(array, rule):
    n_ctx, n_head = lax.axis_size("ctx"), lax.axis_size("head")
    pairs = []
    for c in range(n_ctx):
        for h in range(n_head):
            to = rule(c, h)
            if 0 <= to[0] < n_ctx:
                pairs.append((c * n_head + h, to[0] * n_head + to[1]))
    return lax.ppermute(array, BOTH, pairs)


def in_pair(c, h):
    return (c ^ 1, h)


def even_chain(c, h):
    return (c ^ 2, h)


def odd_chain(c, h):
    return (c + 2, h) if c & 2 else (c - 2, h)


def across(c, h):
    return (c + 1, h) if c & 1 else (c - 1, h)


def forward(c, h):
    if h & 1:
        return (c ^ 1, h)
    return (c - 2, h) if c & 1 else (c + 2, h)


def offsets(pos):
    pair = 1 - 2 * lax.rem(pos, 2)
    chain = 2 - 4 * lax.rem(pos // 2, 2)
    return pair, chain, -chain, -pair


def after(value, *others):
    return lax.optimization_barrier((value,) + others)[0]


def pack_kernel(*refs):
    arrays, out_ref, sems = refs[:-2], refs[-2], refs[-1]
    rows = arrays[0].shape[0]
    copies = [
        pltpu.make_async_copy(ref, out_ref.at[n * rows:(n + 1) * rows], sems.at[n])
        for n, ref in enumerate(arrays)
    ]
    for copy in copies:
        copy.start()
    for copy in copies:
        copy.wait()


def pack(*arrays):
    rows, feat = arrays[0].shape
    count = len(arrays)
    return pl.pallas_call(
        pack_kernel,
        in_specs=[ANY] * count,
        out_specs=VMEM,
        out_shape=jax.ShapeDtypeStruct((count * rows, feat), arrays[0].dtype),
        scratch_shapes=[pltpu.SemaphoreType.DMA((count,))],
        compiler_params=pltpu.CompilerParams(vmem_limit_bytes=VMEM_PACK),
        cost_estimate=pl.CostEstimate(
            flops=0, bytes_accessed=4 * count * rows * feat, transcendentals=0
        ),
    )(*arrays)


def begin_kernel(order_ref, w_ref, g_a, g_b, out_ref, kept_ref, used, sems):
    cols = g_a.shape[1]
    copies = []
    for n in range(4):
        start = pl.multiple_of(order_ref[n] * cols, cols)
        to = used.at[n] if n < 2 else kept_ref.at[:, (n - 2) * cols:(n - 1) * cols]
        copies.append(pltpu.make_async_copy(w_ref.at[:, pl.ds(start, cols)], to, sems.at[n]))
        copies[-1].start()
    copies[0].wait()
    total = dot(used[0], g_a[...], NT)
    copies[1].wait()
    out_ref[...] = total + dot(used[1], g_b[...], NT)
    copies[2].wait()
    copies[3].wait()


def begin_project(order, out_weight, g_a, g_b):
    rows, cols = g_a.shape
    feat = out_weight.shape[0]
    return pl.pallas_call(
        begin_kernel,
        in_specs=[SMEM, ANY, VMEM, VMEM],
        out_specs=[VMEM, VMEM],
        out_shape=[
            jax.ShapeDtypeStruct((feat, rows), jnp.float32),
            jax.ShapeDtypeStruct((feat, 2 * cols), out_weight.dtype),
        ],
        scratch_shapes=[
            pltpu.VMEM((2, feat, cols), out_weight.dtype),
            pltpu.SemaphoreType.DMA((4,)),
        ],
        compiler_params=pltpu.CompilerParams(vmem_limit_bytes=VMEM_ALONE),
        cost_estimate=pl.CostEstimate(
            flops=4 * rows * cols * feat, bytes_accessed=8 * feat * cols, transcendentals=0
        ),
    )(order, out_weight, g_a, g_b)


def end_kernel(w_ref, g_a, g_b, begun, out_ref):
    cols = g_a.shape[1]
    total = begun[...] + dot(w_ref[:, :cols], g_a[...], NT)
    out_ref[...] = (total + dot(w_ref[:, cols:], g_b[...], NT)).astype(out_ref.dtype)


def end_project(weight, g_a, g_b, begun):
    rows, cols = g_a.shape
    feat = weight.shape[0]
    return kernel_call(
        end_kernel,
        jax.ShapeDtypeStruct((feat, rows), jnp.bfloat16),
        [weight, g_a, g_b, begun],
        4 * rows * cols * feat,
    )


def columns(head):
    return slice(head * HEAD_DIM, (head + 1) * HEAD_DIM)


def stat_rows(heads):
    return -(-heads * STATS // STAT_TILE) * STAT_TILE


def block_rows(n, head, rows):
    at = (head * BLOCKS + n) * rows
    return slice(at, at + rows)


def bias_row(live_flags):
    parts = [
        jnp.full((1, TILE), jnp.where(flag, 0.0, -jnp.inf).astype(jnp.float32))
        for flag in live_flags
    ]
    return jnp.concatenate(parts, axis=1)


def bias_kernel(pos_ref, mask_ref, window_ref, source_ref):
    pos = pos_ref[0]
    rows = window_ref.shape[1]
    tiles = rows // TILE
    total_tiles = mask_ref.shape[0]
    window_ref[...] = jnp.zeros_like(window_ref)
    source_ref[...] = jnp.zeros_like(source_ref)
    for n, off in enumerate((0,) + offsets(pos)):
        for b in range(tiles):
            at = slice(n * tiles + b, n * tiles + b + 1)
            column = (off + SPAN) * tiles + b
            window_ref[at, :] = bias_row(
                [mask_ref[pos * tiles + a, column] > 0 for a in range(tiles)]
            )
            flags = []
            for a in range(tiles):
                tile = (pos + off) * tiles + a
                inside = (tile >= 0) & (tile < total_tiles)
                column = (SPAN - off) * tiles + b
                flags.append(inside & (mask_ref[jnp.clip(tile, 0, total_tiles - 1), column] > 0))
            source_ref[at, :] = bias_row(flags)


def biases_of(pos, tile_mask, rows):
    count = -(-(2 * SPAN + 1) * (rows // TILE) // 8) * 8
    shape = jax.ShapeDtypeStruct((count, rows), jnp.float32)
    return kernel_call(bias_kernel, [shape, shape], [pos, tile_mask], 0)


def bias_rows(ref, which):
    tiles = ref.shape[1] // TILE
    return [[ref[n * tiles + b:n * tiles + b + 1, :] for b in range(tiles)] for n in which]


def over_keys(reduce, values):
    return reduce(values.reshape(TILE // 8, 8, values.shape[1]), axis=0)


def softmax_part(scores, biases):
    shifted = []
    top = None
    for block, rows in zip(scores, biases):
        shifted.append([])
        for b, row in enumerate(rows):
            value = block[b * TILE:(b + 1) * TILE] * SCALE_LOG2 + row
            shifted[-1].append(value)
            peak = over_keys(jnp.max, value)
            top = peak if top is None else jnp.maximum(top, peak)
    return shifted, jnp.max(top, axis=0, keepdims=True)


def weighted_values(shifted, top, values_of, keep=None):
    totals = None
    blocks = []
    for n, parts in enumerate(shifted):
        weights = []
        for value in parts:
            weight = jnp.exp2(value - top)
            weights.append(weight)
            part = over_keys(jnp.sum, weight)
            totals = part if totals is None else totals + part
        weights = jnp.concatenate(weights, axis=0)
        if keep is not None:
            keep(n, weights)
        blocks.append(weights.astype(jnp.bfloat16))
    values = jnp.concatenate([values_of(n) for n in range(len(blocks))], axis=0)
    out = dot(values, jnp.concatenate(blocks, axis=0), TN)
    return jnp.sum(totals, axis=0, keepdims=True), out


def in_order(steps, ahead_of, finish):
    ahead = ahead_of(*steps[0])
    for at, step in enumerate(steps):
        now = ahead
        if at + 1 < len(steps):
            ahead = ahead_of(*steps[at + 1])
        finish(*step, now)


def forward_kernel(which, bias_ref, *rest):
    windows, (out_ref, run_ref, kept_ref) = rest[:len(which)], rest[len(which):]
    feat, rows = out_ref.shape
    biases = bias_rows(bias_ref, which)

    def scores_of(head):
        cols = columns(head)
        q = windows[0][2 * rows:, cols]
        return [dot(w[:rows, cols], q, NT) for w in windows]

    def finish(head, scores):
        cols = columns(head)

        def values_of(n):
            return windows[n][rows:2 * rows, cols]

        def keep(n, weights):
            kept_ref[block_rows(n, head, rows), :] = weights

        shifted, top = softmax_part(scores, biases)
        totals, out = weighted_values(shifted, top, values_of, keep)
        out_ref[cols, :] = out
        at = head * RUN_ROWS
        run_ref[at:at + 8, :] = jnp.broadcast_to(top, (8, rows))
        run_ref[at + 8:at + 16, :] = jnp.broadcast_to(totals, (8, rows))

    in_order([(head,) for head in range(feat // HEAD_DIM)], scores_of, finish)


def forward_part(bias, own, which, windows):
    rows, feat = own.shape[0] // 3, own.shape[1]
    heads = feat // HEAD_DIM
    return kernel_call(
        functools.partial(forward_kernel, which),
        [
            jax.ShapeDtypeStruct((feat, rows), jnp.float32),
            jax.ShapeDtypeStruct((heads * RUN_ROWS, rows), jnp.float32),
            jax.ShapeDtypeStruct((len(which) * feat // HEAD_DIM * rows, rows), jnp.float32),
        ],
        [bias, own, *windows],
        4 * len(which) * rows * rows * feat,
        len(which) * rows * rows * heads,
    )


def statistics_kernel(
    which, bias_ref, own_ref, w_ref, out_in, run_in, d_ref, stats_ref, packed_ref
):
    feat, rows = d_ref.shape
    biases = bias_rows(bias_ref, [which])

    def scores_of(head):
        cols = columns(head)
        return [dot(w_ref[:rows, cols], own_ref[2 * rows:, cols], NT)]

    def finish(head, scores):
        cols = columns(head)

        def values_of(n):
            return w_ref[rows:, cols]

        at = head * RUN_ROWS
        top_before, totals_before = run_in[at:at + 1, :], run_in[at + 8:at + 9, :]
        shifted, top = softmax_part(scores, biases)
        top = jnp.maximum(top, top_before)
        totals, out = weighted_values(shifted, top, values_of)
        shrink = jnp.exp2(top_before - top)
        totals = totals + totals_before * shrink
        out = out + out_in[cols, :] * shrink
        attn_out = (out / totals).astype(jnp.bfloat16).astype(jnp.float32)
        delta = jnp.sum(d_ref[cols, :].astype(jnp.float32) * attn_out, axis=0, keepdims=True)
        place = head * STATS
        for stat in (top + jnp.log2(totals), delta):
            for _ in range(3):
                piece = stat.astype(jnp.bfloat16).astype(jnp.float32)
                all_stats[0] = jnp.where(row == place, piece, all_stats[0])
                stat = stat - piece
                place += 1
        packed_ref[cols, :] = d_ref[cols, :]

    row = lax.broadcasted_iota(jnp.int32, stats_ref.shape, 0)
    all_stats = [jnp.zeros(stats_ref.shape, jnp.float32)]
    in_order([(head,) for head in range(feat // HEAD_DIM)], scores_of, finish)
    stats_ref[...] = all_stats[0].astype(jnp.bfloat16)
    packed_ref[feat:, :] = all_stats[0].astype(jnp.bfloat16)


def statistics(bias, own, which, window, out, run, d_out_t):
    feat, rows = d_out_t.shape
    heads = feat // HEAD_DIM
    return kernel_call(
        functools.partial(statistics_kernel, which),
        [
            jax.ShapeDtypeStruct((stat_rows(heads), rows), jnp.bfloat16),
            jax.ShapeDtypeStruct((feat + stat_rows(heads), rows), jnp.bfloat16),
        ],
        [bias, own, window, out, run, d_out_t],
        4 * rows * rows * feat,
        rows * rows * heads,
    )


def statistics_of(ref, start, head):
    stats = ref[start:, :].astype(jnp.float32)
    rows = [stats[head * STATS + n:head * STATS + n + 1] for n in range(STATS)]
    return rows[0] + rows[1] + rows[2], rows[3] + rows[4] + rows[5]


def block_grads(scores, dprobs, bias_rows, lse, delta):
    probs = jnp.concatenate(
        [
            jnp.exp2(scores[b * TILE:(b + 1) * TILE] * SCALE_LOG2 + (row - lse))
            for b, row in enumerate(bias_rows)
        ],
        axis=0,
    )
    dscores = probs * (dprobs - delta)
    return probs.astype(jnp.bfloat16), dscores.astype(jnp.bfloat16)


def query_kernel(which, bias_ref, own_ref, *rest):
    windows, rest = (own_ref,) + rest[:BLOCKS], rest[BLOCKS:]
    d_ref, s_ref, run_ref, kept_ref, q_last, d_last, *outs = rest
    dq_ref, dk_ref, dv_ref, scores_ref, dprobs_ref = outs
    rows, feat = dq_ref.shape
    last_bias = bias_rows(bias_ref, which[BLOCKS:])[0]

    def products(head):
        cols = columns(head)
        keys, values = own_ref[:rows, cols], own_ref[rows:2 * rows, cols]
        queries = own_ref[2 * rows:, cols]
        for n in range(BLOCKS):
            others = q_last[:, cols] if n == BLOCKS - 1 else windows[n + 1][2 * rows:, cols]
            scores_ref[block_rows(n, head, rows), :] = dot(keys, others, NT)
        dprobs_ref[head * rows:(head + 1) * rows, :] = dot(values, d_last[cols, :], NN)
        scores = dot(windows[BLOCKS][:rows, cols], queries, NT)
        return scores, [dot(w[rows:2 * rows, cols], d_ref[cols, :], NN) for w in windows]

    def finish(head, now):
        cols = columns(head)
        scores, dprobs = now
        lse, delta = statistics_of(s_ref, 0, head)
        at = head * RUN_ROWS
        factor = jnp.exp2(run_ref[at:at + 1, :] - lse)
        dscores = []
        for n in range(BLOCKS):
            probs = kept_ref[block_rows(n, head, rows), :] * factor
            dscores.append((probs * (dprobs[n] - delta)).astype(jnp.bfloat16))
            if n == 0:
                dv_ref[:, cols] = dot(probs.astype(jnp.bfloat16), d_ref[cols, :], NT)
        dk_ref[:, cols] = dot(dscores[0], own_ref[2 * rows:, cols], NN)
        dscores.append(block_grads(scores, dprobs[BLOCKS], last_bias, lse, delta)[1])
        keys = jnp.concatenate([w[:rows, cols] for w in windows], axis=0)
        dq = dot(keys, jnp.concatenate(dscores, axis=0), TN)
        dq_ref[:, cols] = jnp.transpose(dq * SCALE).astype(dq_ref.dtype)

    in_order([(head,) for head in range(feat // HEAD_DIM)], products, finish)


def query_side(bias, own, which, windows, d_out_t, stats, run, kept, q_last, d_last):
    feat, rows = d_out_t.shape
    heads = feat // HEAD_DIM
    total = jax.ShapeDtypeStruct((rows, feat), jnp.float32)
    return kernel_call(
        functools.partial(query_kernel, which),
        [
            jax.ShapeDtypeStruct((rows, feat), jnp.bfloat16),
            total,
            total,
            jax.ShapeDtypeStruct((heads * BLOCKS * rows, rows), jnp.float32),
            jax.ShapeDtypeStruct((heads * rows, rows), jnp.float32),
        ],
        [bias, own, *windows, d_out_t, stats, run, kept, q_last, d_last],
        36 * rows * rows * feat,
        rows * rows * heads,
    )


def key_kernel(which, bias_ref, own_ref, *rest):
    sources = [rest[3 * n:3 * n + 3] for n in range(BLOCKS)]
    scores_ref, dprobs_ref, dk_in, dv_in, dk_out, dv_out, dk_ref, dv_ref, sems = rest[3 * BLOCKS:]
    copies = []
    rows, feat = dk_in.shape
    biases = bias_rows(bias_ref, which)

    def products(head):
        cols = columns(head)
        values = own_ref[rows:2 * rows, cols]
        dprobs = [dot(values, sources[n][1][cols, :], NN) for n in range(BLOCKS - 1)]
        return dprobs + [dprobs_ref[head * rows:(head + 1) * rows, :]]

    def finish(head, dprobs):
        cols = columns(head)
        blocks = []
        for n, (_, _, s_ref) in enumerate(sources):
            start = feat if s_ref.shape[0] > feat else 0
            scores = scores_ref[block_rows(n, head, rows), :]
            blocks.append(
                block_grads(scores, dprobs[n], biases[n], *statistics_of(s_ref, start, head))
            )
        probs, dscores = (jnp.concatenate(parts, axis=1) for parts in zip(*blocks))
        queries = jnp.concatenate([q[q.shape[0] - rows:, cols] for q, _, _ in sources], axis=0)
        grads = jnp.concatenate([d[cols, :] for _, d, _ in sources], axis=1)
        dk = dk_in[:, cols] + dot(dscores, queries, NN)
        dv = dv_in[:, cols] + dot(probs, grads, NT)
        dk_ref[:, cols] = (dk * SCALE).astype(dk_ref.dtype)
        dv_ref[:, cols] = dv.astype(dv_ref.dtype)
        for which_out, (from_ref, to_ref) in enumerate(((dk_ref, dk_out), (dv_ref, dv_out))):
            copies.append(
                pltpu.make_async_copy(
                    from_ref.at[:, cols], to_ref.at[:, cols], sems.at[2 * head + which_out]
                )
            )
            copies[-1].start()

    in_order([(head,) for head in range(feat // HEAD_DIM)], products, finish)
    for copy in copies:
        copy.wait()


def key_side(bias, own, sources, scores, dprobs, begun):
    rows, feat = begun[0].shape
    operands = [bias, own]
    for _, q, d, s in sources:
        operands += [q, d, s]
    operands += [scores, dprobs, *begun]
    return pl.pallas_call(
        functools.partial(key_kernel, [source[0] for source in sources]),
        in_specs=[VMEM] * len(operands),
        out_specs=[ANY] * 2,
        out_shape=[jax.ShapeDtypeStruct((rows, feat), jnp.bfloat16)] * 2,
        scratch_shapes=[
            pltpu.VMEM((rows, feat), jnp.bfloat16),
            pltpu.VMEM((rows, feat), jnp.bfloat16),
            pltpu.SemaphoreType.DMA((2 * feat // HEAD_DIM,)),
        ],
        compiler_params=pltpu.CompilerParams(vmem_limit_bytes=VMEM_LIMIT),
        cost_estimate=pl.CostEstimate(
            flops=26 * rows * rows * feat,
            bytes_accessed=sum(x.size * x.dtype.itemsize for x in operands),
            transcendentals=BLOCKS * rows * rows * feat // HEAD_DIM,
        ),
    )(*operands)


def local(queries, keys, values, out_weight, reward_grad, tile_mask):
    rows = queries.shape[0]
    ctx = lax.axis_index("ctx").astype(jnp.int32)
    head = lax.axis_index("head").astype(jnp.int32)
    pos = ctx.reshape(1)

    def second_step(x, a, b):
        a_is_held = (ctx % 2 == 0) == (ctx // 2 % 2 == 0)
        return jnp.where(head % 2 == 1, jnp.where(a_is_held, a, b), x)

    far = send(reward_grad, lambda c, h: (c, h ^ 2))
    kvq = pack(keys, values, queries)
    kvq_b = send(kvq, odd_chain)
    kvq_a = send(kvq, even_chain)
    kvq_x = send(kvq, in_pair)
    near = send(after(reward_grad, kvq), lambda c, h: (c, h ^ 1))
    order = jnp.stack([head, head ^ 1, head ^ 2, head ^ 3])
    own_bias, other_bias = biases_of(pos, tile_mask, rows)
    near = after(near, own_bias, other_bias)
    begun, kept = begin_project(order, out_weight, reward_grad, near)
    far = after(far, begun)
    far_near = send(far, lambda c, h: (c, h ^ 1))
    second = second_step(kvq_x, kvq_a, kvq_b)
    kv_g = send(second[:2 * rows], forward)
    d_out_t = end_project(kept, far, far_near, after(begun, second))
    out, run, kept_weights = forward_part(
        own_bias, kvq, [0, 1, 3, 2], [kvq_x, kvq_b, kvq_a]
    )
    stats, packed = statistics(own_bias, kvq, 4, kv_g, out, run, d_out_t)
    q_g = send(second[2 * rows:], forward)
    d_g = send(d_out_t, across)
    p_b = send(packed, odd_chain)
    p_a = send(packed, even_chain)
    p_x = send(packed, in_pair)
    s_g = send(stats, across)
    grad_queries, *begun_keys, scores, dprobs = query_side(
        own_bias, kvq, [0, 1, 3, 2, 4], [kvq_x, kvq_b, kvq_a, kv_g], d_out_t,
        stats, run, kept_weights, q_g, d_g,
    )
    grad_keys, grad_values = key_side(
        other_bias,
        kvq,
        [
            (1, kvq_x, p_x, p_x),
            (3, kvq_b, p_b, p_b),
            (2, kvq_a, p_a, p_a),
            (4, q_g, d_g, s_g),
        ],
        scores,
        dprobs,
        begun_keys,
    )
    return (grad_queries, grad_keys, grad_values)


def solution(mesh):
    placed = (
        P("ctx", "head"),
        P("ctx", "head"),
        P("ctx", "head"),
        P("head", None),
        P("ctx", "head"),
        P(),
    )
    return jax.shard_map(
        local,
        mesh=mesh,
        in_specs=placed,
        out_specs=(P("ctx", "head"), P("ctx", "head"), P("ctx", "head")),
        check_vma=False,
    )
```
